32 devices in a mesh: batch: 16 (over z, y, x), rep: 2 (over core).
Axes of the slice: x: 2, y: 2, z: 4, core: 2. Of those that a mesh axis runs over, the one named last changes fastest.
Arguments:
- obs_latent: float32 [2048, 50], P(('batch', 'rep')), may hold values from -6 to 6
- actions: float32 [2048, 10, 6], P(('batch', 'rep')), may hold values from -1 to 1
- next_latent: float32 [2048, 10, 50], P(('batch', 'rep')), may hold values from -6 to 6
- reward_target: float32 [2048, 10], P(('batch', 'rep')), may hold values from -6 to 6
- value_target: float32 [2048, 10], P(('batch', 'rep')), may hold values from -6 to 6
- lengths: int32 [2048], P(('batch', 'rep')), may hold values from 0 to 10, as said below
- first_weight: float32 [2, 56, 2048], replicated, may hold values from -0.75 to 0.75
- opening_layer_offset: float32 [2, 2048], replicated, may hold values from -1.5 to 1.5
- mid_weight: float32 [2, 4, 512, 512], replicated, may hold values from -0.25 to 0.25
- mid_bias: float32 [2, 4, 512], replicated, may hold values from -1.5 to 1.5
- norm_gain: float32 [2, 2, 512], replicated, may hold values from 0.25 to 1.75
- norm_bias: float32 [2, 2, 512], replicated, may hold values from -1.5 to 1.5
- latent_out: float32 [2, 512, 50], replicated, may hold values from -0.25 to 0.25
- latent_bias: float32 [2, 50], replicated, may hold values from -1.5 to 1.5
- payoff_critic_projection: float32 [2, 3, 512], replicated, may hold values from -0.25 to 0.25
- scalar_bias: float32 [2, 3], replicated, may hold values from -2 to 2
- obs_gain: float32 [50], replicated, may hold values from 0.5 to 2
- plan_start: float32 [2, 50], P('rep'), may hold values from -6 to 6
- action_guess_average: float32 [2, 5, 6], P('rep'), may hold values from -0.5 to 0.5
- plan_init_std: float32 [2, 5, 6], P('rep'), may hold values from 0.3 to 1
- action_noise: float32 [2, 6, 64, 5, 6], P('rep', None, 'batch'), may hold values from -4 to 4
- elite_index: int32 [2, 6, 8], P('rep'), may hold values from 0 to 63, as said below
Outputs:
- grad_first_weight: float32 [2, 56, 2048], replicated
- grad_first_bias: float32 [2, 2048], replicated
- grad_mid_weight: float32 [2, 4, 512, 512], replicated
- grad_mid_bias: float32 [2, 4, 512], replicated
- gradient_norm_gain: float32 [2, 2, 512], replicated
- grad_norm_bias: float32 [2, 2, 512], replicated
- grad_latent_out: float32 [2, 512, 50], replicated
- grad_latent_bias: float32 [2, 50], replicated
- grad_scalar_out: float32 [2, 3, 512], replicated
- grad_scalar_bias: float32 [2, 3], replicated
- grad_obs_gain: float32 [50], replicated
- grad_obs_latent: float32 [2048, 50], P(('batch', 'rep'))
- plan_mean: float32 [2, 5, 6], P('rep')
- plan_std: float32 [2, 5, 6], P('rep')
The draws below stay inside these ranges and needn't reach their ends.
Inputs may be any that keep to these rules, and one draw needn't show every extreme that they name: `lengths`: 0 marks an empty slot; the first of every 64 slots in a row holds 10 transitions. `elite_index`: the 8 numbers of one environment and iteration differ.
All inputs are finite; a program needn't handle non-finite values.
Results may differ from the reference program's by a relative error of at most 0.0003.
Values sent between devices are 32-bit elements; how exact they have to be, the bound alone decides.
No kernel may reach another device: no remote copies, remote signals or barrier semaphores. Data moves between devices by JAX's collectives and lax.ppermute only.
A program may use at most 256 MiB of HBM per device.

```python
import math
import jax
import jax.numpy as jnp
from jax import lax

Z = 50
A = 6
HID = 512
LAYERS = 2
H = 10
HP = 5
ITERS = 6
SLOTS = 64
SLOTS_ALL = 2048
SAMPLES = 64
ELITES = 8
ENVS = 2


def draw_next_latent(key, part):
    key = jax.random.fold_in(key, 7)
    rough_key, common_key = jax.random.split(key)
    rough = jnp.clip(jax.random.normal(rough_key, (SLOTS_ALL, H, Z), jnp.float32), -4.0, 4.0)
    common = jax.random.uniform(common_key, (Z,), jnp.float32, -2.0, 2.0)
    return rough + common[None, None, :]


def draw_lengths(key, part):
    key = jax.random.fold_in(key, 11)
    drawn = jax.random.randint(key, (SLOTS_ALL,), 0, H + 1)
    leading = jnp.arange(SLOTS_ALL) % SLOTS == 0
    return jnp.where(leading, H, drawn).astype(jnp.int32)


def draw_elite_index(key, part):
    key = jax.random.fold_in(key, 23)
    subkeys = jax.random.split(key, ENVS * ITERS)

    def pick_elites(subkey):
        return jax.random.permutation(subkey, SAMPLES)[:ELITES]
    picked = jax.vmap(pick_elites)(subkeys)
    return picked.reshape(ENVS, ITERS, ELITES).astype(jnp.int32)


def shard_levels(rng, shape, shards, low, largest):
    level = 1.0
    for dim, parts in shards:
        steps = jax.random.uniform(jax.random.fold_in(jax.random.fold_in(rng, 6), dim), (parts,), jnp.float32, low / len(shards), largest / len(shards))
        level = level * jnp.repeat(jnp.exp(steps), shape[dim] // parts).reshape((-1,) + (1,) * (len(shape) - 1 - dim))
    return level


def gaussian(stream_key, dims, deviation, reach, cuts=(), held_as=jnp.bfloat16):
    factor_of = shard_levels(stream_key, dims, cuts, -0.22, 0.18) if cuts else 1.0
    entries = jax.random.normal(stream_key, dims, jnp.float32) * deviation * factor_of
    return jnp.minimum(jnp.maximum(entries, -reach), reach).astype(held_as)


def setup_inputs(seed: int = 0) -> dict:
    streams_of = jax.random.split(jax.random.key(seed), 23)
    return {
        "obs_latent": gaussian(streams_of[0], (SLOTS_ALL, Z), 1.0, 6.0, ((0, 32),), jnp.float32),
        "actions": jnp.clip(jax.random.uniform(streams_of[1], (SLOTS_ALL, H, A), jnp.float32, -1.0, 1.0) * shard_levels(streams_of[1], (SLOTS_ALL, H, A), ((0, 32),), -0.4, 0.0), -1.0, 1.0),
        "next_latent": draw_next_latent(jax.random.fold_in(streams_of[22], 71), 0),
        "reward_target": gaussian(streams_of[3], (SLOTS_ALL, H), 1.0, 6.0, ((0, 32),), jnp.float32),
        "value_target": gaussian(streams_of[4], (SLOTS_ALL, H), 1.0, 6.0, ((0, 32),), jnp.float32),
        "lengths": draw_lengths(jax.random.fold_in(streams_of[22], 71), 0),
        "first_weight": gaussian(streams_of[6], (LAYERS, Z + A, 4 * HID), (Z + A) ** -0.5, 0.75, (), jnp.float32),
        "opening_layer_offset": gaussian(streams_of[7], (LAYERS, 4 * HID), 0.3, 1.5, (), jnp.float32),
        "mid_weight": gaussian(streams_of[8], (LAYERS, 4, HID, HID), HID ** -0.5, 0.25, (), jnp.float32),
        "mid_bias": gaussian(streams_of[9], (LAYERS, 4, HID), 0.3, 1.5, (), jnp.float32),
        "norm_gain": jnp.clip(1.0 + 0.15 * jax.random.normal(streams_of[10], (LAYERS, 2, HID), jnp.float32), 0.25, 1.75),
        "norm_bias": gaussian(streams_of[11], (LAYERS, 2, HID), 0.3, 1.5, (), jnp.float32),
        "latent_out": gaussian(streams_of[12], (LAYERS, HID, Z), HID ** -0.5, 0.25, (), jnp.float32),
        "latent_bias": gaussian(streams_of[13], (LAYERS, Z), 0.3, 1.5, (), jnp.float32),
        "payoff_critic_projection": gaussian(streams_of[14], (LAYERS, 3, HID), HID ** -0.5, 0.25, (), jnp.float32),
        "scalar_bias": gaussian(streams_of[15], (LAYERS, 3), 0.5, 2.0, (), jnp.float32),
        "obs_gain": jnp.clip(jnp.exp(jax.random.uniform(streams_of[16], (Z,), jnp.float32, math.log(0.5), math.log(2.0))), 0.5, 2.0),
        "plan_start": gaussian(streams_of[17], (ENVS, Z), 1.0, 6.0, ((0, 2),), jnp.float32),
        "action_guess_average": jnp.clip(jax.random.uniform(streams_of[18], (ENVS, HP, A), jnp.float32, -0.5, 0.5) * shard_levels(streams_of[18], (ENVS, HP, A), ((0, 2),), -0.4, 0.0), -0.5, 0.5),
        "plan_init_std": jnp.clip(0.3 + 0.7 * jax.random.uniform(streams_of[19], (ENVS, HP, A), jnp.float32) ** shard_levels(streams_of[19], (ENVS, HP, A), ((0, 2),), -0.2, 0.2), 0.3, 1.0),
        "action_noise": gaussian(streams_of[20], (ENVS, ITERS, SAMPLES, HP, A), 1.0, 4.0, ((0, 2), (2, 16)), jnp.float32),
        "elite_index": draw_elite_index(jax.random.fold_in(streams_of[22], 71), 0),
    }


@jax.custom_vjp
def low(v):
    return lax.optimization_barrier(v.astype(jnp.bfloat16)).astype(jnp.float32)

@jax.custom_vjp
def low_back(v):
    return v

def low_keep(v):
    return (low(v), None)

def low_pass(kept, grad):
    return (grad,)

def back_keep(v):
    return (v, None)

def back_low(kept, grad):
    return (low(grad),)
low.defvjp(low_keep, low_pass)
low_back.defvjp(back_keep, back_low)
highest = lax.Precision.HIGHEST
rho_decay = 0.5
consistency_coef = 2.0
reward_coef = 0.5
value_coef = 0.1
discount = 0.99
exponent_sharpness_level = 4.0
std_floor = 0.1
norm_epsilon = 1e-05
lowest_score = -1e+30

def latent_step(params, latent, action):
    first_weight, opening_layer_offset, mid_weight, mid_bias, norm_gain, norm_bias, latent_out, latent_bias, payoff_critic_projection, scalar_bias = params
    reward = 0.0
    value_one = 0.0
    value_two = 0.0
    for layer_index in range(first_weight.shape[0]):
        joined = jnp.concatenate([latent, action], axis=-1)
        opening = jnp.dot(joined, first_weight[layer_index], precision=highest) + opening_layer_offset[layer_index]
        opening = opening.reshape(opening.shape[0], 4, -1)
        activated = jax.nn.elu(opening[:, 0:2])
        value_pre = opening[:, 2:4]
        centered = value_pre - lax.optimization_barrier(jnp.mean(value_pre, axis=-1, keepdims=True))
        variance = lax.optimization_barrier(jnp.mean(centered * centered, axis=-1, keepdims=True))
        normed = jnp.tanh(centered * lax.rsqrt(variance + norm_epsilon) * norm_gain[layer_index] + norm_bias[layer_index])
        hiddens = jnp.concatenate([activated, normed], axis=1)
        middle = jax.nn.elu(jnp.einsum('nkh,khg->nkg', hiddens, mid_weight[layer_index], precision=highest) + mid_bias[layer_index])
        latent = latent + jnp.dot(middle[:, 0], latent_out[layer_index], precision=highest) + latent_bias[layer_index]
        outputs = jnp.einsum('nkh,kh->nk', middle[:, 1:4], payoff_critic_projection[layer_index], precision=highest) + scalar_bias[layer_index]
        reward = reward + outputs[:, 0]
        value_one = value_one + outputs[:, 1]
        value_two = value_two + outputs[:, 2]
    return (latent, reward, value_one, value_two)

def sequence_loss(params, obs_gain, obs_latent, actions, next_latent, reward_target, value_target, lengths):
    slots = obs_latent.shape[0]
    horizon = actions.shape[1]
    latent = obs_latent * obs_gain
    positions = jnp.arange(horizon, dtype=jnp.int32)
    live = (positions[None, :] < lengths[:, None]).astype(latent.dtype)
    factors = jnp.power(jnp.asarray(rho_decay, latent.dtype), positions.astype(latent.dtype))

    def advance(current, inputs):
        action, target_latent, target_reward, target_value, alive, factor = inputs
        moved, reward, value_one, value_two = latent_step(params, current, action)
        differ = moved - target_latent
        reward_miss = reward - target_reward
        miss_one = value_one - target_value
        miss_two = value_two - target_value
        terms = consistency_coef * lax.optimization_barrier(jnp.mean(differ * differ, axis=-1)) + reward_coef * reward_miss * reward_miss + value_coef * (miss_one * miss_one + miss_two * miss_two)
        return (moved, jnp.sum(alive * terms) * factor)
    inputs = (jnp.swapaxes(actions, 0, 1), jnp.swapaxes(next_latent, 0, 1), reward_target.T, value_target.T, live.T, factors)
    _, losses = lax.scan(advance, latent, inputs)
    return jnp.sum(losses) / (slots * horizon)

def plan_returns(params, latent, sampled):
    horizon = sampled.shape[1]
    returns = jnp.zeros((latent.shape[0],), latent.dtype)
    for position in range(horizon):
        latent, reward, value_one, value_two = latent_step(params, latent, sampled[:, position])
        returns = returns + discount ** position * reward
    return returns + discount ** (horizon - 1) * jnp.minimum(value_one, value_two)

def plan_search(params, plan_start, action_guess_average, plan_init_std, action_noise, elite_index):
    envs = action_noise.shape[0]
    iterations = action_noise.shape[1]
    samples = action_noise.shape[2]
    sample_ids = jnp.arange(samples, dtype=jnp.int32)
    plan_mean = action_guess_average
    plan_std = plan_init_std
    for iteration in range(iterations):
        sampled = jnp.tanh(plan_mean[:, None] + plan_std[:, None] * action_noise[:, iteration])
        latents = jnp.broadcast_to(plan_start[:, None, :], (envs, samples, plan_start.shape[-1])).reshape(envs * samples, -1)
        returns = plan_returns(params, latents, sampled.reshape((envs * samples,) + sampled.shape[2:])).reshape(envs, samples)
        flagged_items = jnp.any(sample_ids[None, :, None] == elite_index[:, iteration][:, None, :], axis=-1)
        hidden_out_ratings = jnp.where(flagged_items, returns, lowest_score)
        peak_discounted_payoff = lax.optimization_barrier(jnp.max(hidden_out_ratings, axis=-1))
        candidate_importance_list = jnp.where(flagged_items, jnp.exp(exponent_sharpness_level * (hidden_out_ratings - peak_discounted_payoff[:, None])), 0.0)
        weight_sum = lax.optimization_barrier(jnp.sum(candidate_importance_list, axis=-1))
        plan_mean = jnp.einsum('es,espa->epa', candidate_importance_list, sampled, precision=highest) / weight_sum[:, None, None]
        centered = sampled - plan_mean[:, None]
        variance = jnp.einsum('es,espa->epa', candidate_importance_list, centered * centered, precision=highest) / weight_sum[:, None, None]
        plan_std = jnp.sqrt(variance + std_floor * std_floor)
    return (plan_mean, plan_std)

def reference(obs_latent, actions, next_latent, reward_target, value_target, lengths, first_weight, opening_layer_offset, mid_weight, mid_bias, norm_gain, norm_bias, latent_out, latent_bias, payoff_critic_projection, scalar_bias, obs_gain, plan_start, action_guess_average, plan_init_std, action_noise, elite_index):
    params = (first_weight, opening_layer_offset, mid_weight, mid_bias, norm_gain, norm_bias, latent_out, latent_bias, payoff_critic_projection, scalar_bias)
    groups = obs_latent.shape[0] // SLOTS

    def regroup(array):
        return array.reshape((groups, SLOTS) + array.shape[1:])
    blocks = (regroup(obs_latent), regroup(actions), regroup(next_latent), regroup(reward_target), regroup(value_target), regroup(lengths))

    def group_pass(carry, block):

        def local_loss(candidate_importance_list, gain, latent_in):
            return sequence_loss(candidate_importance_list, gain, latent_in, block[1], block[2], block[3], block[4], block[5])
        result, pullback = jax.vjp(local_loss, params, obs_gain, block[0])
        weight_grads, gain_grad, latent_grad = pullback(jnp.ones_like(result))
        carry = jax.tree.map(jnp.add, carry, (weight_grads, gain_grad))
        return (carry, latent_grad)
    initial = jax.tree.map(jnp.zeros_like, (params, obs_gain))
    (weight_grads, gain_grad), latent_grads = lax.scan(group_pass, initial, blocks)
    grad_obs_latent = latent_grads.reshape(obs_latent.shape)

    def trajectory_planner(candidate_importance_list):
        return plan_search(candidate_importance_list, plan_start, action_guess_average, plan_init_std, action_noise, elite_index)
    (plan_mean, plan_std), _ = jax.vjp(trajectory_planner, params)
    return (weight_grads[0], weight_grads[1], weight_grads[2], weight_grads[3], weight_grads[4], weight_grads[5], weight_grads[6], weight_grads[7], weight_grads[8], weight_grads[9], gain_grad, grad_obs_latent, plan_mean, plan_std)
```

```python
import functools

import jax
import jax.numpy as jnp
from jax import lax
from jax.experimental import pallas as pl
from jax.experimental.pallas import tpu as pltpu
from jax.sharding import PartitionSpec as P

F32 = jnp.float32
BF16 = jnp.bfloat16

rho_decay = 0.5
consistency_coef = 2.0
reward_coef = 0.5
value_coef = 0.1
discount = 0.99
exponent_sharpness_level = 4.0
std_floor = 0.1
norm_epsilon = 1e-05

G = 64
W = 256
ONE = 56
REWARD = 57
VALUE = 58
COEF = 59
LENGTH = 60
START = 61
CHUNKS = 8
ROW_BLOCK = 208
SHORT = 2 * ROW_BLOCK
GATHERED = 512
HEAD_LIMIT = 34
BACK_LIMIT = 20

bf = functools.partial(jax.ShapeDtypeStruct, dtype=BF16)
f32 = functools.partial(jax.ShapeDtypeStruct, dtype=F32)


def dot(a, b):
    return jnp.dot(a, b, preferred_element_type=F32)


def dot_rows(a, b):
    return lax.dot_general(a, b, (((0,), (0,)), ((), ())), preferred_element_type=F32)


def split(v):
    high = v.astype(BF16)
    return high, (v - high.astype(F32)).astype(BF16)


def dot_split(high, low, w_high, w_low):
    n = high.shape[0]
    both = dot(jnp.concatenate([high, low], axis=0), w_high)
    return both[:n] + (both[n:] + dot(high, w_low))


def elu(v):
    return jnp.where(v > 0, v, jnp.exp(jnp.minimum(v, 0.0)) - 1.0)


def elu_slope(out):
    return jnp.where(out > 0, 1.0, out + 1.0)


def lanes(shape):
    return lax.broadcasted_iota(jnp.int32, shape, len(shape) - 1)


def sublanes(shape):
    return lax.broadcasted_iota(jnp.int32, shape, len(shape) - 2)


def pack_input(x):
    high = x.astype(BF16).astype(F32)
    lane = lanes(x.shape)
    low_group = (lane >= G) & (lane < 2 * G)
    return jnp.where(low_group, x - high, high).astype(BF16)


def three_groups(v):
    v = jnp.where(lanes(v.shape) < G, v, 0.0)
    return jnp.concatenate([v + pltpu.roll(v, G, 1), v], axis=1)


def padded_first(weight, bias):
    shape = (8, weight.shape[1])
    extra = jnp.where(sublanes(shape) == 0, jnp.broadcast_to(bias, shape), 0.0)
    return jnp.concatenate([weight, extra], axis=0)


def store_packed(ref, layer, full):
    high, low = split(full)
    ref[layer, 0:G, :] = high
    ref[layer, G : 2 * G, :] = high
    ref[layer, 2 * G : 3 * G, :] = low
    ref[layer, 3 * G : W, :] = jnp.zeros_like(high)


def position():
    b = lax.axis_index("batch")
    return b & 1, (b >> 1) & 1, lax.axis_index("rep")


def noise_place(n):
    return slice(n // 4 * 8, n // 4 * 8 + 8), slice(n % 4 * 128, n % 4 * 128 + 128)


def forward_kernel(
    next_ref, act_ref, obs_ref, rew_ref, val_ref, len_ref, gain_ref, noise_ref, elite_ref,
    w1_ref, b1_ref, wm_ref, bm_ref, wo_ref, bo_ref,
    xs, xc_ref, cc_ref, pt_ref, count_ref, misc_ref, noise_out, hhs, hls, mhs, mls, pulls, *refs
):
    outs, (feat, wide, line, parts), splits, sems = refs[:5], refs[5:9], refs[9:14], refs[14]
    w1p, wmh, wml, woh, wol = splits
    copies = [pltpu.make_async_copy(a, b, sems.at[n]) for n, (a, b) in enumerate(zip(splits, outs))]
    horizon, latent, slots = next_ref.shape
    width = act_ref.shape[1]
    layers = w1_ref.shape[0]

    iterations, steps, samples, _ = noise_ref.shape
    elites = elite_ref.shape[2]
    base = lax.axis_index("batch") * samples
    line[...] = jnp.zeros_like(line)
    noise_out[...] = jnp.zeros_like(noise_out)
    square = (elites, elites)
    for i in range(iterations):
        chosen = jnp.broadcast_to(elite_ref[i], square)
        mine = jnp.max(jnp.where(lanes(square) == sublanes(square), chosen, -1), axis=1, keepdims=True)
        total = jnp.zeros((elites, 128), F32)
        for t in range(steps):
            line[0:samples, 0:width] = noise_ref[i, t]
            part = jnp.zeros((elites, 128), F32)
            for j in range(samples):
                row = jnp.broadcast_to(line[j : j + 1, :], (elites, 128))
                part = part + jnp.where(mine == base + j, row, 0.0)
            total = total + (pltpu.roll(part, t * width, 1) if t else part)
        for e in range(elites // 8):
            noise_out[noise_place(i * (elites // 8) + e)] = total[e * 8 : e * 8 + 8]

    wide[...] = jnp.zeros_like(wide)
    line[...] = jnp.zeros_like(line)
    for l in range(layers):
        store_packed(w1p, l, padded_first(w1_ref[l], b1_ref[l : l + 1, :]))
        wmh[l], wml[l] = split(wm_ref[l, 0])
        for g in range(3):
            wide[g * G : g * G + latent, :] = wo_ref[:, l, :]
        woh[l], wol[l] = split(wide[...].T)
    for copy in copies:
        copy.start()
    line[...] = jnp.zeros_like(line)
    line[0:1, 0:latent] = gain_ref[...]
    line[1 : 1 + layers, 0:latent] = bo_ref[...]
    small = three_groups(line[0:8, :])
    misc_ref[slots : slots + 8, :] = small

    def turned():
        v = feat[...].T
        return jnp.concatenate([v, jnp.where(lanes(v.shape) < G, v, 0.0)], axis=1)

    feat[...] = jnp.zeros_like(feat)
    for g in range(2):
        feat[g * G : g * G + latent, :] = obs_ref[...]
    obs = turned()
    misc_ref[0:slots, :] = obs
    for g in range(2):
        feat[g * G + ONE : g * G + ONE + 1, :] = jnp.ones((1, slots), F32)

    lengths = len_ref[...].astype(F32)
    before = jnp.where(sublanes((slots, slots)) < lanes((slots, slots)), 1.0, 0.0).astype(BF16)
    starts = dot(jnp.broadcast_to(lengths, (16, slots)).astype(BF16), before)[0:1]
    count = jnp.sum(lengths, axis=1, keepdims=True)
    count_ref[...] = jnp.broadcast_to(count, count_ref.shape)
    for g in range(2):
        feat[g * G + LENGTH : g * G + LENGTH + 1, :] = lengths
        feat[g * G + START : g * G + START + 1, :] = starts
    place = lanes((slots, pt_ref.shape[1]))

    lane = lanes((slots, W))
    part = lane % G
    is_latent = (part < latent) & (lane < 3 * G)
    is_target = (lane[:, 0:128] >= REWARD) & (lane[:, 0:128] <= COEF)
    is_input = (part >= latent) & (part <= ONE) & (lane < 3 * G)

    def step(t, carry):
        z, factor = carry
        coef = jnp.where(t < len_ref[...], factor, 0.0)
        for g in range(2):
            at = g * G
            feat[at : at + latent, :] = next_ref[t]
            feat[at + latent : at + latent + width, :] = act_ref[t]
            feat[at + REWARD : at + REWARD + 1, :] = rew_ref[pl.ds(t, 1), :]
            feat[at + VALUE : at + VALUE + 1, :] = val_ref[pl.ds(t, 1), :]
            feat[at + COEF : at + COEF + 1, :] = coef
        cond = turned()
        rows = pl.ds(pl.multiple_of(t * slots, slots), slots)
        live = t.astype(F32) < cond[:, LENGTH : LENGTH + 1]
        at = jnp.where(live, cond[:, START : START + 1] + t.astype(F32), -1.0).astype(jnp.int32)
        pt_ref[rows, :] = jnp.where(place == at, 1.0, 0.0).astype(BF16)
        rest = jnp.where(is_target, cond[:, 0:128], 0.0)
        packed = 0.0
        for n in range(3):
            high = rest.astype(BF16).astype(F32)
            rest = rest - high
            packed = packed + (pltpu.roll(high, 8 * n, 1) if n else high)
        parts[rows, :] = packed.astype(BF16)
        u = jnp.where(is_input, cond, 0.0)
        for l in range(layers):
            xp = pack_input(z + u)
            xs[l, rows, :] = xp
            high, low = split(elu(dot(xp, w1p[l])))
            hhs[l, rows, :] = high
            hls[l, rows, :] = low
            high, low = split(elu(dot_split(high, low, wmh[l], wml[l]) + bm_ref[l, 0:1, :]))
            mhs[l, rows, :] = high
            mls[l, rows, :] = low
            z = z + dot_split(high, low, woh[l], wol[l]) + small[1 + l : 2 + l, :]
        scale = (2.0 * consistency_coef / latent) * cond[:, COEF : COEF + 1]
        pulls[rows, :] = jnp.where(is_latent, scale * (z - cond), 0.0)
        return z, factor * rho_decay

    lax.fori_loop(0, horizon, step, (obs * small[0:1, :], jnp.float32(1.0 / (slots * horizon))))


    def gather(top, size):
        at = slice(top, top + size)
        found = dot_rows(pt_ref[:, at], jnp.concatenate([xs[l] for l in range(layers)] + [parts[...]], axis=1))
        for l in range(layers):
            xc_ref[l, at, :] = found[:, l * W : (l + 1) * W].astype(BF16)
        values = found[:, layers * W :]
        cc_ref[at, :] = values + (pltpu.roll(values, 120, 1) + pltpu.roll(values, 112, 1))

    gather(0, GATHERED)

    @pl.when(jnp.max(count) > SHORT)
    def _():
        gather(GATHERED, pt_ref.shape[1] - GATHERED)

    for copy in copies:
        copy.wait()


def send_halves(g, keep_ref, send_ref):
    core = lax.axis_index("rep")
    half = CHUNKS // 2
    keep_ref[...] = g[:, pl.ds(core * half, half)]
    send_ref[...] = g[:, pl.ds((1 - core) * half, half)]


def weight_grads(g, layer, xp, hh, hl, dph, dpl, doh, dol, extra):
    hidden = hh.shape[1]
    grad = dot_rows(hh, dph) + (dot_rows(hl, dph) + dot_rows(hh, dpl))
    rows = hidden // CHUNKS
    for c in range(CHUNKS):
        g[layer, c, 0:rows, :] = grad[c * rows : (c + 1) * rows]
    x = xp[:, 0 : 2 * G]
    both = dot_rows(x, doh) + dot_rows(x, dol)
    first = both[0:G] + both[G : 2 * G]
    for c in range(CHUNKS):
        part = first[c * 8 : c * 8 + 8]
        g[layer, c, rows : rows + 8, :] = part if c < CHUNKS - 1 else part + extra


def turn_weights(w1_ref, b1_ref, wm_ref, wo_ref, w1th, w1tl, wmth, wmtl, wotp, wide):
    latent = wo_ref.shape[0]
    wide[...] = jnp.zeros_like(wide)
    for l in range(w1_ref.shape[0]):
        full = padded_first(w1_ref[l], b1_ref[l : l + 1, :])
        turned = jnp.concatenate([full, full, full, jnp.zeros_like(full)], axis=0).T
        w1th[l], w1tl[l] = split(turned)
        wmth[l], wmtl[l] = split(wm_ref[l, 0].T)
        wide[0:latent, :] = wo_ref[:, l, :]
        store_packed(wotp, l, wide[...])


def heads_kernel(head, has_dx, turns, *refs):
    if turns:
        *refs, wide = refs
        dynamics = refs[11 + has_dx : 15 + has_dx]
        out = len(refs) - 16 - 5
        turn_weights(*dynamics, *refs[out : out + 5], wide)
        refs = refs[:out] + refs[out + 5 :]

    (xp_ref, cond_ref, count_ref, w1_ref, b1_ref, wm_ref, bm_ref, ng_ref, nb_ref, p_ref, sb_ref) = refs[:11]
    refs = refs[11:]
    dx_in = refs[0] if has_dx else None
    refs = refs[1:] if has_dx else refs
    (
        keep_ref, send_ref, dx_ref, w1_out, wmh_out, wml_out,
        w1p, wmh, wml, w1th, w1tl, wmth, wmtl, hh, hl, dph, dpl, doh, dol, sums, g, sems,
    ) = refs[len(refs) - 22 :]
    layers = xp_ref.shape[0]
    capacity = hh.shape[1]
    short = jnp.max(count_ref[...]) <= SHORT
    blocks = jnp.where(short, SHORT // ROW_BLOCK, capacity // ROW_BLOCK)
    for l in range(layers):
        dx_ref[l, SHORT:, :] = jnp.zeros((dx_ref.shape[1] - SHORT, W), F32)
    is_reward = head == 1
    target_lane = REWARD if is_reward else VALUE
    scale = 2.0 * (reward_coef if is_reward else value_coef)
    for l in range(layers):
        full = padded_first(w1_ref[l], b1_ref[l : l + 1, :])
        store_packed(w1p, l, full)
        turned = jnp.concatenate([full, full, full, jnp.zeros_like(full)], axis=0).T
        w1th[l], w1tl[l] = split(turned)
        wm = wm_ref[l, 0]
        wmh[l], wml[l] = split(wm)
        wmth[l], wmtl[l] = split(wm.T)
    weights = [
        pltpu.make_async_copy(src, dst, sems.at[n])
        for n, (src, dst) in enumerate(((w1p, w1_out), (wmh, wmh_out), (wml, wml_out)))
    ]
    for copy in weights:
        copy.start()
    sums[...] = jnp.zeros_like(sums)

    def block(i, carry):
        rows = pl.ds(pl.multiple_of(i * ROW_BLOCK, ROW_BLOCK), ROW_BLOCK)
        kept = []
        score = 0.0
        for l in range(layers):
            o = dot(xp_ref[l, rows, :], w1p[l])
            if is_reward:
                h = elu(o)
                norm = None
            else:
                centered = o - jnp.mean(o, axis=-1, keepdims=True)
                variance = jnp.mean(centered * centered, axis=-1, keepdims=True)
                scale_rows = lax.rsqrt(variance + norm_epsilon)
                unit = centered * scale_rows
                gain = ng_ref[l, head - 2 : head - 1, :]
                h = jnp.tanh(unit * gain + nb_ref[l, head - 2 : head - 1, :])
                norm = (unit, scale_rows, gain)
            high, low = split(h)
            hh[l, rows, :] = high
            hl[l, rows, :] = low
            m = elu(dot_split(high, low, wmh[l], wml[l]) + bm_ref[l, head : head + 1, :])
            p = p_ref[head - 1, l : l + 1, :]
            score = score + jnp.sum(m * p, axis=-1, keepdims=True) + sb_ref[l, head - 1]
            kept.append((h, norm, m, p))
        cond = cond_ref[rows, :]
        miss = score - cond[:, target_lane : target_lane + 1]
        dscore = (scale * cond[:, COEF : COEF + 1]) * miss
        dscore_sum = jnp.sum(dscore, axis=0, keepdims=True)
        for l in range(layers):
            h, norm, m, p = kept[l]
            dp = jnp.sum(dscore * m, axis=0, keepdims=True)
            dpre = (dscore * p) * elu_slope(m)
            dbm = jnp.sum(dpre, axis=0, keepdims=True)
            high, low = split(dpre)
            dph[l, rows, :] = high
            dpl[l, rows, :] = low
            dh = dot_split(high, low, wmth[l], wmtl[l])
            if is_reward:
                do = dh * elu_slope(h)
            else:
                unit, scale_rows, gain = norm
                dn = dh * (1.0 - h * h)
                sums[l, 2:3, :] += jnp.sum(dn * unit, axis=0, keepdims=True)
                sums[l, 3:4, :] += jnp.sum(dn, axis=0, keepdims=True)
                dunit = dn * gain
                do = scale_rows * (
                    dunit
                    - jnp.mean(dunit, axis=-1, keepdims=True)
                    - unit * jnp.mean(dunit * unit, axis=-1, keepdims=True)
                )
            sums[l, 1:2, :] += dbm
            sums[l, 4:5, :] += dp
            sums[l, 5:6, :] += jnp.broadcast_to(dscore_sum, (1, sums.shape[2]))
            high, low = split(do)
            doh[l, rows, :] = high
            dol[l, rows, :] = low
            dx = dot_split(high, low, w1th[l], w1tl[l])
            dx_ref[l, rows, :] = dx_in[l, rows, :] + dx if has_dx else dx
        return carry

    lax.fori_loop(0, blocks, block, 0)

    def finish(n):
        for l in range(layers):
            rows = [ref[l, 0:n, :] for ref in (hh, hl, dph, dpl, doh, dol)]
            weight_grads(g, l, xp_ref[l, 0:n, :], *rows, sums[l])

    pl.when(short)(functools.partial(finish, SHORT))
    pl.when(jnp.logical_not(short))(functools.partial(finish, capacity))
    send_halves(g, keep_ref, send_ref)
    for copy in weights:
        copy.wait()


def backward_kernel(
    xp_ref, hh_ref, hl_ref, mh_ref, ml_ref, pull_ref, dx_ref, misc_ref,
    w1th, w1tl, wmth, wmtl, wotp, pt_ref, count_ref, *rest
):
    keep_ref, send_ref, dobs_ref, dxs, dph, dpl, doh, dol, dzs, sums, g = rest[len(rest) - 11 :]
    layers, rows_all = xp_ref.shape[0], xp_ref.shape[1]
    latent, slots = dobs_ref.shape
    horizon = rows_all // slots
    hidden = wmth.shape[-1]
    sums[...] = jnp.zeros_like(sums)

    def scatter(n):
        parts = [split(dx_ref[l, 0:n, :]) for l in range(layers)]
        found = dot(pt_ref[:, 0:n], jnp.concatenate([v for pair in parts for v in pair], axis=1))
        for l in range(layers):
            at = 2 * l * W
            dxs[l] = found[:, at : at + W] + found[:, at + W : at + 2 * W]

    short = jnp.max(count_ref[...]) <= SHORT
    pl.when(short)(functools.partial(scatter, GATHERED))
    pl.when(jnp.logical_not(short))(functools.partial(scatter, pt_ref.shape[1]))
    lane = lanes((slots, W))
    is_latent = ((lane % G) < latent) & (lane < 3 * G)

    def step(i, dz):
        t = horizon - 1 - i
        rows = pl.ds(pl.multiple_of(t * slots, slots), slots)
        dz = dz + pull_ref[rows, :]
        for l in reversed(range(layers)):
            dzp = pack_input(dz)
            dzs[l, rows, :] = dzp[:, 0 : 2 * G]
            sums[l, 2:3, 0:W] += jnp.sum(dz, axis=0, keepdims=True)
            m = mh_ref[l, rows, :].astype(F32) + ml_ref[l, rows, :].astype(F32)
            dpre = dot(dzp, wotp[l]) * elu_slope(m)
            sums[l, 1:2, :] += jnp.sum(dpre, axis=0, keepdims=True)
            high, low = split(dpre)
            dph[l, rows, :] = high
            dpl[l, rows, :] = low
            h = hh_ref[l, rows, :].astype(F32) + hl_ref[l, rows, :].astype(F32)
            do = dot_split(high, low, wmth[l], wmtl[l]) * elu_slope(h)
            high, low = split(do)
            doh[l, rows, :] = high
            dol[l, rows, :] = low
            dx = dot_split(high, low, w1th[l], w1tl[l]) + dxs[l, rows, :]
            dz = dz + jnp.where(is_latent, dx, 0.0)
        return dz

    dz = lax.fori_loop(0, horizon, step, jnp.zeros((slots, W), F32))
    dobs_ref[...] = (dz * misc_ref[slots : slots + 1, :])[:, 0:128].T[0:latent]
    sums[0, 3:4, 0:W] = jnp.sum(dz * misc_ref[0:slots, :], axis=0, keepdims=True)
    rows = hidden // CHUNKS
    for l in range(layers):
        weight_grads(g, l, xp_ref.at[l], hh_ref[l], hl_ref[l], dph[l], dpl[l], doh[l], dol[l], sums[l])
        both = dot_rows(dzs[l], mh_ref[l]) + dot_rows(dzs[l], ml_ref[l])
        out = both[0:G] + both[G : 2 * G]
        for c in range(CHUNKS):
            g[l, c, rows + 8 : rows + 16, :] = out[c * 8 : c * 8 + 8]
    send_halves(g, keep_ref, send_ref)


def planner_kernel(iteration, first, *refs):
    weights = refs[:14]
    state_in = refs[14:17] if first else refs[14:15]
    refs = refs[17:] if first else refs[15:]
    (noise_ref, misc_ref, bm_ref, ng_ref, nb_ref, p_ref, sb_ref) = refs[:7]
    out_ref, xs, acts, line = refs[len(refs) - 4 :]
    w1p, wmh, wml = weights[0:4], weights[4:8], weights[8:12]
    woh, wol = weights[12:14]
    horizon, elites = acts.shape[0], acts.shape[1]
    layers = w1p[0].shape[0]
    slots = misc_ref.shape[0] - 8
    latent = 50

    lane = lanes((1, W))
    is_action = ((lane % G) >= latent) & ((lane % G) < ONE) & (lane < 3 * G)
    is_one = ((lane % G) == ONE) & (lane < 3 * G)
    group = lane // G

    def placed(v, at):
        return jnp.where(is_action, three_groups(pltpu.roll(v, (latent - at) % 128, 1)), 0.0)

    def three(v):
        high = v.astype(BF16)
        rest = v - high.astype(F32)
        mid = rest.astype(BF16)
        return high, mid, (rest - mid.astype(F32)).astype(BF16)

    def dot_fine(v, w_high, w_low):
        n = v.shape[0]
        high, mid, low = three(v)
        a = dot(jnp.concatenate([high, mid, low], axis=0), w_high)
        b = dot(jnp.concatenate([high, mid], axis=0), w_low)
        return a[0:n] + (a[n : 2 * n] + b[0:n] + (a[2 * n : 3 * n] + b[n : 2 * n]))

    def dot_first(x, w):
        n = x.shape[0]
        high, mid, low = three(x)
        keep = (group == 0) | (group == 2)
        zero = jnp.zeros_like(high)
        high = jnp.where(keep, high, zero)
        mid = jnp.where(keep, mid, zero)
        low = jnp.where(group == 0, low, zero)
        a = dot(jnp.concatenate([high, mid, low], axis=0), w)
        return a[0:n] + (a[n : 2 * n] + a[2 * n : 3 * n])

    def middle(h, l, k):
        return elu(dot_fine(h, wmh[k][l], wml[k][l]) + bm_ref[l, k : k + 1, :])

    def head(m, l, k):
        return jnp.sum(m * p_ref[k - 1, l : l + 1, :], axis=-1, keepdims=True) + sb_ref[l, k - 1]

    def value(x, l, k):
        o = dot_first(x, w1p[k][l])
        centered = o - jnp.mean(o, axis=-1, keepdims=True)
        variance = jnp.mean(centered * centered, axis=-1, keepdims=True)
        unit = centered * lax.rsqrt(variance + norm_epsilon)
        h = jnp.tanh(unit * ng_ref[l, k - 2 : k - 1, :] + nb_ref[l, k - 2 : k - 1, :])
        return head(middle(h, l, k), l, k)

    if first:
        mean_ref, std_ref, start_ref = state_in
        line[...] = jnp.zeros_like(line)
        line[0:horizon, 0:6] = mean_ref[...]
        line[8 : 8 + horizon, 0:6] = std_ref[...]
        line[16:17, 0:latent] = start_ref[...]
        for t in range(horizon):
            out_ref[0, t : t + 1, :] = placed(line[t : t + 1, :], 0)
            out_ref[1, t : t + 1, :] = placed(line[8 + t : 9 + t, :], 0)
        out_ref[2, 0:1, :] = three_groups(line[16:17, :])
        state_ref = out_ref
    else:
        (state_ref,) = state_in
        out_ref[2] = state_ref[2]

    tiles = elites // 8
    noise = [noise_ref[noise_place(iteration * tiles + e)] for e in range(tiles)]
    noise = jnp.concatenate(noise, axis=0) if tiles > 1 else noise[0]
    for t in range(horizon):
        acts[t] = jnp.where(
            is_action,
            jnp.tanh(state_ref[0, t : t + 1, :] + state_ref[1, t : t + 1, :] * placed(noise, 6 * t)),
            0.0,
        )
    z = jnp.broadcast_to(state_ref[2, 0:1, :], (elites, W))
    for t in range(horizon):
        u = jnp.where(is_one, 1.0, acts[t])
        for l in range(layers):
            x = z + u
            xs[l, t] = x
            if t < horizon - 1 or l < layers - 1:
                m = middle(elu(dot_first(x, w1p[0][l])), l, 0)
                z = z + dot_fine(m, woh[l], wol[l]) + misc_ref[slots + 1 + l : slots + 2 + l, :]
    reward = 0.0
    one = 0.0
    two = 0.0
    for l in range(layers):
        x = xs[l].reshape(horizon * elites, W)
        reward = reward + head(middle(elu(dot_first(x, w1p[1][l])), l, 1), l, 1)
        x = xs[l, horizon - 1]
        one = one + value(x, l, 2)
        two = two + value(x, l, 3)
    returns = discount ** (horizon - 1) * jnp.minimum(one, two)
    for t in range(horizon):
        returns = returns + discount**t * reward[t * elites : (t + 1) * elites]
    top = jnp.max(returns, axis=0, keepdims=True)
    weight = jnp.exp(exponent_sharpness_level * (returns - top))
    total = jnp.sum(weight, axis=0, keepdims=True)
    for t in range(horizon):
        sampled = acts[t]
        mean = jnp.sum(weight * sampled, axis=0, keepdims=True) / total
        centered = sampled - mean
        variance = jnp.sum(weight * (centered * centered), axis=0, keepdims=True) / total
        out_ref[0, t : t + 1, :] = mean
        out_ref[1, t : t + 1, :] = jnp.sqrt(variance + std_floor * std_floor)


CORE = 0


def bits():
    x, y, _ = position()
    return ((x, y, lambda f, s: f + 2 * s), (y, x, lambda f, s: 2 * f + s))


def first_partner(l):
    return (1, 2)[l]


def second_partner(l):
    return (2, 1)[l]


def blocks(ref, rows):
    def at(n):
        return ref.at[pl.ds(n * rows, rows)]

    return at


def add_first(rows, ins, keeps, sends):
    keep, recv = (blocks(r, rows) for r in ins)
    kept = blocks(keeps[0], rows)
    for l, (f, _, chunk) in enumerate(bits()):
        sent = blocks(sends[l], rows)
        for m in range(2):
            mine, other = 4 * l + chunk(f, m), 4 * l + chunk(1 - f, m)
            kept(2 * l + m)[...] = keep(mine)[...] + recv(mine)[...]
            sent(m)[...] = keep(other)[...] + recv(other)[...]


def add_second(rows, ins, keeps, sends):
    keep, kept = blocks(ins[0], rows), blocks(keeps[0], rows)
    for l, (_, s, _) in enumerate(bits()):
        recv = blocks(ins[1 + l], rows)
        kept(l)[...] = keep(2 * l + s)[...] + recv(s)[...]
        sends[l][...] = keep(2 * l + 1 - s)[...] + recv(1 - s)[...]


def add_third(rows, ins, keeps, sends):
    for l in range(2):
        at = slice(l * rows, l * rows + rows)
        total = ins[0][at] + ins[1 + l][...]
        for ref in (*keeps, *sends):
            ref[at] = total


def add_whole(rows, ins, keeps, sends):
    total = ins[0][...]
    for ref in ins[1:]:
        total = total + ref[...]
    for ref in (*keeps, *sends):
        ref[...] = total


def add_last(rows, ins, keeps, sends):
    total = ins[0][...] + ins[1][...]
    keeps[0][...] = total
    for l in range(2):
        sends[l][...] = total[l * rows : l * rows + rows]


def join_two(rows, ins, keeps, sends):
    kept = blocks(keeps[0], rows)
    for l, (_, s, _) in enumerate(bits()):
        own, sent = ins[0][l * rows : l * rows + rows], blocks(sends[l], rows)
        recv = ins[1 + l][...]
        for at, value in ((s, own), (1 - s, recv)):
            kept(2 * l + at)[...] = value
            sent(at)[...] = value


def join_four(rows, ins, keeps, sends):
    own = blocks(ins[0], rows)
    for l, (f, _, chunk) in enumerate(bits()):
        recv = blocks(ins[1 + l], rows)
        for m in range(2):
            for at, value in ((chunk(f, m), own(2 * l + m)[...]), (chunk(1 - f, m), recv(m)[...])):
                for ref in (*keeps, *sends):
                    blocks(ref, rows)(4 * l + at)[...] = value


class Received:
    def __init__(self, buffer, start, rows):
        self.buffer, self.start, self.rows = buffer, start, rows


class Sums:
    def __init__(self, batch):
        self.batch = batch
        self.pending = []
        self.after = []
        self.late = []

    def swap(self, a, partner):
        if partner == CORE:
            return lax.ppermute(a, "rep", [(0, 1), (1, 0)])
        return lax.ppermute(a, "batch", [(i, i ^ partner) for i in range(self.batch)])

    def start(self, steps, done):
        self.pending.append([steps, done, next(steps)])

    def advance(self):
        if not self.pending:
            return
        jobs = [entry[2] for entry in self.pending]
        arrays, buffers = [], {}
        for _, _, ins, _, sends in jobs:
            for a in ins:
                a = a.buffer if isinstance(a, Received) else a
                if not any(a is b for b in arrays):
                    arrays.append(a)
            for partner, rows in sends:
                buffers[partner] = buffers.get(partner, 0) + rows
        partners = list(buffers)
        width = jobs[0][2][0].shape[-1]
        out_shape = [f32((n, width)) for _, _, _, keeps, _ in jobs for n in keeps]
        out_shape += [f32((buffers[p], width)) for p in partners] + [f32((8, 128))]
        after = self.after + self.late

        def kernel(*refs):
            ins_all, outs = refs[: len(arrays)], list(refs[len(arrays) + len(after) :])
            outs.pop()[...] = jnp.zeros((8, 128), F32)
            sent_refs = dict(zip(partners, outs[len(outs) - len(partners) :]))
            used = dict.fromkeys(partners, 0)
            for fn, rows, ins, keeps, sends in jobs:
                in_refs = []
                for a in ins:
                    whole = a.buffer if isinstance(a, Received) else a
                    ref = ins_all[[whole is b for b in arrays].index(True)]
                    in_refs.append(ref.at[pl.ds(a.start, a.rows)] if isinstance(a, Received) else ref)
                sent = []
                for partner, n in sends:
                    sent.append(sent_refs[partner].at[pl.ds(used[partner], n)])
                    used[partner] += n
                fn(rows, in_refs, outs[: len(keeps)], sent)
                outs = outs[len(keeps) :]

        outs = pl.pallas_call(
            kernel,
            in_specs=[vmem()] * len(arrays) + [hbm()] * len(after),
            out_specs=[vmem()] * len(out_shape),
            out_shape=out_shape,
            compiler_params=params(20),
            cost_estimate=cost(1),
            name="add_up",
        )(*arrays, *after)
        token = outs[-1]
        received = {p: self.swap(a, p) for p, a in zip(partners, outs[len(outs) - 1 - len(partners) :])}
        used = dict.fromkeys(partners, 0)
        self.late = []
        for entry, (_, _, _, keeps, sends) in zip(list(self.pending), jobs):
            result = list(outs[: len(keeps)])
            outs = outs[len(keeps) :]
            for partner, n in sends:
                result.append(Received(received[partner], used[partner], n))
                used[partner] += n
            try:
                entry[2] = entry[0].send(result)
            except StopIteration as stop:
                self.pending.remove(entry)
                entry[1].append(stop.value)
                if isinstance(stop.value[-1], Received):
                    self.late.append(stop.value[-1].buffer)
        self.after = [token]

    def sum_small(self, a):
        rows, bit, steps = a.shape[0], 4, []
        while bit < self.batch:
            steps.append(bit)
            bit *= 2
        steps += [1, 2]
        recv = self.swap(a, steps[0])
        for partner in steps[1:]:
            a, recv = yield (add_whole, rows, (a, recv), (rows,), ((partner, rows),))
        (a,) = yield (add_whole, rows, (a, recv), (rows,), ())
        return (a,)

    def sum_batch(self, keep, send):
        _, _, rows, hidden = keep.shape
        keep, send = keep.reshape(-1, hidden), send.reshape(-1, hidden)
        to_first = tuple((first_partner(l), 2 * rows) for l in range(2))
        to_second = tuple((second_partner(l), rows) for l in range(2))
        keep, ra, rb = yield (add_first, rows, (keep, self.swap(send, CORE)), (4 * rows,), to_first)
        keep, ra, rb = yield (add_second, rows, (keep, ra, rb), (2 * rows,), to_second)
        keep, recv = yield (add_third, rows, (keep, ra, rb), (2 * rows,), ((4, 2 * rows),))
        bit = 8
        while bit < self.batch:
            keep, recv = yield (add_whole, rows, (keep, recv), (2 * rows,), ((bit, 2 * rows),))
            bit *= 2
        keep, ra, rb = yield (add_last, rows, (keep, recv), (2 * rows,), to_second)
        keep, ra, rb = yield (join_two, rows, (keep, ra, rb), (4 * rows,), to_first)
        keep, recv = yield (join_four, rows, (keep, ra, rb), (8 * rows,), ((CORE, 8 * rows),))
        return rows, keep, recv


def vmem():
    return pl.BlockSpec(memory_space=pltpu.VMEM)


def smem():
    return pl.BlockSpec(memory_space=pltpu.SMEM)


def hbm():
    return pl.BlockSpec(memory_space=pl.ANY)


def params(mebibytes):
    return pltpu.CompilerParams(vmem_limit_bytes=mebibytes * 1024 * 1024)


def in_hbm(a):
    return pltpu.with_memory_space_constraint(a, pltpu.HBM)


def cost(us):
    return pl.CostEstimate(flops=int(us * 1e9), bytes_accessed=0, transcendentals=0)


def shape_of(a):
    return jax.ShapeDtypeStruct(a.shape, a.dtype)


def assemble_kernel(hidden, latent, batches, *refs):
    half = CHUNKS // 2
    parts, heights = {}, {}
    for n, (k, height, start) in enumerate(batches):
        parts[k] = [refs[2 * n], refs[2 * n + 1].at[pl.ds(start, height * CHUNKS)]]
        heights[k] = height
    last = 0 in parts
    core = lax.axis_index("rep")
    rows = hidden // CHUNKS
    copies = []
    if last:
        small_in, dobs_in = refs[2 * len(batches) + 2 : 2 * len(batches) + 4]
        (
            mid_ref, first_ref, bias_ref, mid_bias_ref, ng_ref, nb_ref, wo_ref, bo_ref, p_ref, sb_ref, gain_ref,
            dobs_ref, sems,
        ) = refs[len(refs) - 13 :]
        dobs_ref[...] = dobs_in[...]
    else:
        mid_ref, first_ref, small_ref, sems = refs[len(refs) - 4 :]

    def copy(src, dst, sem, when=None):
        made = pltpu.make_async_copy(src, dst, sem)
        if when is None:
            made.start()
        else:
            pl.when(when)(made.start)
        return made

    for k in parts:
        at = pl.ds(k * hidden, hidden)
        for l in range(2):
            for m, owner in ((0, core), (1, 1 - core)):
                for j in range(half):
                    top = (l * half + j) * heights[k]
                    src = parts[k][m].at[pl.ds(top, rows)]
                    copies.append(copy(src, mid_ref.at[l, k, owner * half + j], sems.at[0, k, l, m, j]))
                    rest = parts[k][m].at[pl.ds(top + rows, 8)]
                    lower = copy(rest, first_ref.at[l, j, :, at], sems.at[1, k, l, 0, j], owner == 0)
                    if m == 0:
                        copies.append(lower)
                    if j < half - 1:
                        upper = copy(rest, first_ref.at[l, half + j, :, at], sems.at[1, k, l, 1, j], owner == 1)
                        if m == 0:
                            copies.append(upper)

    def chunk(k, l, c, lo, hi):
        top = (l * half + c % half) * heights[k] + rows
        own, other = (parts[k][m][top + lo : top + hi, :] for m in range(2))
        return jnp.where(core == c // half, own, other)

    if last:
        for l in range(2):
            for k in range(4):
                small = chunk(k, l, CHUNKS - 1, 0, 8) if k in parts else small_in[k, l]
                bias_ref[l : l + 1, k * hidden : (k + 1) * hidden] = small[0:1]
                mid_bias_ref[l, k : k + 1, :] = small[1:2]
                if k >= 1:
                    p_ref[k - 1, l : l + 1, :] = small[4:5]
                    sb_ref[l : l + 1, k - 1 : k] = small[5:6, 0:1]
                if k >= 2:
                    ng_ref[l, k - 2 : k - 1, :] = small[2:3]
                    nb_ref[l, k - 2 : k - 1, :] = small[3:4]
                if k == 0:
                    bo_ref[l : l + 1, :] = small[2:3, 0:latent]
                    if l == 0:
                        gain_ref[...] = small[3:4, 0:latent]
            for c in range(CHUNKS - 1):
                n = min(8, latent - 8 * c)
                wo_ref[8 * c : 8 * c + n, l, :] = chunk(0, l, c, 8, 8 + n)
    else:
        small_ref[...] = jnp.zeros_like(small_ref)
        for k in parts:
            for l in range(2):
                small_ref[k, l] = chunk(k, l, CHUNKS - 1, 0, 8)
    for made in copies:
        made.wait()


def shards(
    obs_latent, actions, next_latent, reward_target, value_target, lengths,
    first_weight, opening_layer_offset, mid_weight, mid_bias, norm_gain, norm_bias,
    latent_out, latent_bias, payoff_critic_projection, scalar_bias, obs_gain,
    plan_start, action_guess_average, plan_init_std, action_noise, elite_index,
    *, batch,
):
    slots, latent = obs_latent.shape
    horizon, width = actions.shape[1], actions.shape[2]
    layers, hidden = first_weight.shape[0], mid_weight.shape[-1]
    rows_all = slots * horizon
    joint = latent + width
    iterations, samples_local, plan_horizon = action_noise.shape[1:4]
    elites = elite_index.shape[-1]
    heads = 3
    sums = Sums(batch)

    projection = jnp.transpose(payoff_critic_projection, (1, 0, 2))
    wout = jnp.transpose(latent_out, (2, 0, 1))

    def column(k):
        return [
            pl.BlockSpec((layers, joint, hidden), lambda i: (0, 0, k)),
            pl.BlockSpec((layers, hidden), lambda i: (0, k)),
            pl.BlockSpec((layers, 1, hidden, hidden), lambda i: (0, k, 0, 0)),
        ]

    def scratch(*shape, dtype=BF16):
        return pltpu.VMEM(shape, dtype)

    def copies(*shapes):
        return [scratch(*v.shape, dtype=v.dtype) for v in shapes]

    def to_hbm(*shapes):
        return [pltpu.HBM(v.shape, v.dtype) for v in shapes]

    def weights_of(*arrays):
        return [in_hbm(a) for a in arrays]

    square = bf((layers, hidden, hidden))
    narrow = bf((layers, hidden, W))
    packed = bf((layers, W, hidden))
    wide_rows = bf((layers, rows_all, hidden))
    noise_shape = f32((8 * -(-iterations * (elites // 8) // 4), hidden))
    kept = [packed, square, square, narrow, narrow]
    capacity = -(-rows_all // ROW_BLOCK) * ROW_BLOCK
    gathered = -(-capacity // 128) * 128
    (xp, xc, cc, pt, live_count, misc, noise, hh, hl, mh, ml, pull, w1p, wmh, wml, woh, wol) = pl.pallas_call(
        forward_kernel,
        grid=(1,),
        in_specs=[vmem()] * 9 + column(0) + [vmem()] * 3,
        out_specs=[vmem()] * 12 + [hbm()] * 5,
        out_shape=[
            bf((layers, rows_all, W)), bf((layers, gathered, W)), f32((gathered, 128)), bf((rows_all, gathered)),
            f32((8, 128)), f32((slots + 8, W)), noise_shape,
            *[wide_rows] * 4, f32((rows_all, W)), *to_hbm(*kept),
        ],
        scratch_shapes=[
            scratch(2 * G, slots, dtype=F32),
            scratch(W, hidden, dtype=F32),
            scratch(max(8, samples_local), 128, dtype=F32),
            scratch(rows_all, 128),
            *copies(*kept),
            pltpu.SemaphoreType.DMA((5,)),
        ],
        compiler_params=params(26),
        cost_estimate=cost(20),
        name="forward_chain",
    )(
        *weights_of(
            jnp.transpose(next_latent, (1, 2, 0)), jnp.transpose(actions, (1, 2, 0)), obs_latent.T,
            reward_target.T, value_target.T, lengths[None], obs_gain[None],
            jnp.transpose(action_noise[0], (0, 2, 1, 3)), jnp.transpose(elite_index, (1, 0, 2)),
            first_weight, opening_layer_offset, mid_weight, mid_bias, wout, latent_bias,
        )
    )
    noise_done = []
    sums.start(sums.sum_small(noise), noise_done)
    split_weights = [(w1p, wmh, wml)]

    summed = [[] for _ in range(4)]
    dx = None
    rows = hidden // CHUNKS + 8
    half = f32((layers, CHUNKS // 2, rows, hidden))
    for head in range(1, 1 + heads):
        has_dx = dx is not None
        turns = head == heads
        keep, send, dx, *weights = pl.pallas_call(
            functools.partial(heads_kernel, head, has_dx, turns),
            grid=(1,),
            in_specs=[vmem()] * 3 + column(head) + [vmem()] * 4 + [smem()] + [vmem()] * has_dx
            + (column(0) + [vmem()] if turns else []) + [hbm()] * len(sums.after),
            out_specs=[vmem()] * 3 + [hbm()] * 3 + [vmem()] * (5 * turns),
            out_shape=[half, half, f32((layers, gathered, W)), *to_hbm(packed, square, square)]
            + [narrow, narrow, square, square, packed] * turns,
            scratch_shapes=[
                *copies(packed, square, square, narrow, narrow, square, square),
                *[scratch(layers, capacity, hidden)] * 6,
                scratch(layers, 8, hidden, dtype=F32),
                scratch(layers, CHUNKS, rows, hidden, dtype=F32),
                pltpu.SemaphoreType.DMA((3,)),
                *[scratch(G, hidden, dtype=F32)] * turns,
            ],
            compiler_params=params(HEAD_LIMIT),
            cost_estimate=cost(15),
            name=f"head_{head}",
        )(
            xc, cc, live_count,
            *weights_of(
                first_weight, opening_layer_offset, mid_weight, mid_bias,
                norm_gain, norm_bias, projection, scalar_bias,
            ),
            *([dx] if has_dx else []),
            *(weights_of(first_weight, opening_layer_offset, mid_weight, wout) if turns else []), *sums.after,
        )
        split_weights.append(tuple(weights[:3]))
        turned = weights[3:]
        sums.after = [dx]
        sums.advance()
        sums.start(sums.sum_batch(keep, send), summed[head])

    rows = hidden // CHUNKS + 16
    half = f32((layers, CHUNKS // 2, rows, hidden))
    keep, send, dobs = pl.pallas_call(
        backward_kernel,
        grid=(1,),
        in_specs=[vmem()] * 15 + [hbm()] * len(sums.after),
        out_specs=[vmem()] * 3,
        out_shape=[half, half, f32((latent, slots))],
        scratch_shapes=[
            scratch(layers, rows_all, W, dtype=F32),
            *[scratch(layers, rows_all, hidden)] * 4,
            scratch(layers, rows_all, 2 * G),
            scratch(layers, 8, hidden, dtype=F32),
            scratch(layers, CHUNKS, rows, hidden, dtype=F32),
        ],
        compiler_params=params(BACK_LIMIT),
        cost_estimate=cost(25),
        name="backward_chain",
    )(xp, hh, hl, mh, ml, pull, dx, misc, *turned, pt, live_count, *sums.after)
    sums.after = [dobs]
    sums.advance()
    sums.start(sums.sum_batch(keep, send), summed[0])

    while not noise_done:
        sums.advance()
    ((noise,),) = noise_done
    flat_weights = [w[n] for n in range(3) for w in split_weights] + [woh, wol]
    state = [action_guess_average[0], plan_init_std[0], plan_start]
    for i in range(iterations):
        state = [
            pl.pallas_call(
                functools.partial(planner_kernel, i, i == 0),
                in_specs=[vmem()] * (14 + len(state)) + [vmem()] * 6 + [smem()]
                + [hbm()] * len(sums.after),
                out_specs=vmem(),
                out_shape=f32((3, plan_horizon, W)),
                scratch_shapes=[
                    scratch(layers, plan_horizon, elites, W, dtype=F32),
                    scratch(plan_horizon, elites, W, dtype=F32),
                    scratch(24, 128, dtype=F32),
                ],
                compiler_params=params(20),
                cost_estimate=cost(9),
                name=f"planner_{i}",
            )(
                *flat_weights, *state, noise, misc, mid_bias, norm_gain, norm_bias, projection,
                scalar_bias, *sums.after,
            )
        ]
        sums.after = [state[0]]
        sums.advance()
    plan = state[0][:2, None, :, latent:joint]
    big = [
        f32((layers, 4, CHUNKS, hidden // CHUNKS, hidden)), f32((layers, CHUNKS - 1, 8, 4 * hidden)),
    ]

    def assemble(heads_done, more, out_shape, aliases, name, after):
        done = [(k, *summed[k][0]) for k in heads_done]
        pieces = [p for _, _, own, other in done for p in (own, other.buffer)]
        spec = tuple((k, rows, other.start) for k, rows, _, other in done)
        return pl.pallas_call(
            functools.partial(assemble_kernel, hidden, latent, spec),
            in_specs=[vmem()] * len(pieces) + [hbm(), hbm(), vmem(), vmem()][: len(more)] + [hbm()] * len(after),
            out_specs=[hbm(), hbm()] + [vmem()] * (len(out_shape) - 2),
            out_shape=out_shape,
            scratch_shapes=[pltpu.SemaphoreType.DMA((2, 4, 2, 2, CHUNKS // 2))],
            input_output_aliases={len(pieces) + n: n for n in range(2)} if aliases else {},
            compiler_params=params(24),
            cost_estimate=cost(3),
            name=name,
        )(*pieces, *more, *after)

    early = [k for k in range(4) if summed[k]]
    held = assemble(early, [], big + [f32((4, layers, 8, hidden))], False, "assemble_early", sums.after)
    sums.after = [held[2]]
    while sums.pending:
        sums.advance()
    late = [k for k in range(4) if k not in early]
    mids, firsts, *outs = assemble(
        late,
        [*held, dobs],
        big
        + [
            f32(opening_layer_offset.shape), f32(mid_bias.shape), f32(norm_gain.shape), f32(norm_bias.shape),
            f32(wout.shape), f32(latent_bias.shape), f32(projection.shape), f32(scalar_bias.shape), f32((1, latent)),
            f32(dobs.shape),
        ],
        True,
        "assemble",
        sums.after,
    )
    return (
        firsts.reshape(first_weight.shape),
        outs[0],
        mids.reshape(mid_weight.shape),
        *outs[1:4],
        jnp.transpose(outs[4], (1, 2, 0)),
        outs[5],
        jnp.transpose(outs[6], (1, 0, 2)),
        outs[7],
        outs[8][0],
        outs[9].T,
        plan[0],
        plan[1],
    )


def solution(mesh):
    rows = ("batch", "rep")
    return jax.shard_map(
        functools.partial(shards, batch=mesh.shape["batch"]),
        mesh=mesh,
        in_specs=(
            P(rows, None), P(rows, None, None), P(rows, None, None), P(rows, None), P(rows, None), P(rows),
            P(), P(), P(), P(), P(), P(), P(), P(), P(), P(), P(),
            P("rep", None), P("rep", None, None), P("rep", None, None),
            P("rep", None, "batch", None, None), P("rep", None, None),
        ),
        out_specs=(P(),) * 11 + (P(rows, None), P("rep", None, None), P("rep", None, None)),
        check_vma=False,
    )
```

```python
import functools

import jax
import jax.numpy as jnp
from jax import lax
from jax.experimental import pallas as pl
from jax.experimental.pallas import tpu as pltpu
from jax.sharding import PartitionSpec as P

F32 = jnp.float32
BF16 = jnp.bfloat16

rho_decay = 0.5
consistency_coef = 2.0
reward_coef = 0.5
value_coef = 0.1
discount = 0.99
exponent_sharpness_level = 4.0
std_floor = 0.1
norm_epsilon = 1e-05

G = 64
W = 256
ONE = 56
REWARD = 57
VALUE = 58
COEF = 59
LENGTH = 60
START = 61
CHUNKS = 8
ROW_BLOCK = 208
SHORT = 2 * ROW_BLOCK
GATHERED = 512
HEAD_LIMIT = 34
BACK_LIMIT = 20

bf = functools.partial(jax.ShapeDtypeStruct, dtype=BF16)
f32 = functools.partial(jax.ShapeDtypeStruct, dtype=F32)


def dot(a, b):
    return jnp.dot(a, b, preferred_element_type=F32)


def dot_rows(a, b):
    return lax.dot_general(a, b, (((0,), (0,)), ((), ())), preferred_element_type=F32)


def split(v):
    high = v.astype(BF16)
    return high, (v - high.astype(F32)).astype(BF16)


def dot_split(high, low, w_high, w_low):
    n = high.shape[0]
    both = dot(jnp.concatenate([high, low], axis=0), w_high)
    return both[:n] + (both[n:] + dot(high, w_low))


def elu(v):
    return jnp.where(v > 0, v, jnp.exp(jnp.minimum(v, 0.0)) - 1.0)


def elu_slope(out):
    return jnp.where(out > 0, 1.0, out + 1.0)


def lanes(shape):
    return lax.broadcasted_iota(jnp.int32, shape, len(shape) - 1)


def sublanes(shape):
    return lax.broadcasted_iota(jnp.int32, shape, len(shape) - 2)


def pack_input(x):
    high = x.astype(BF16).astype(F32)
    lane = lanes(x.shape)
    low_group = (lane >= G) & (lane < 2 * G)
    return jnp.where(low_group, x - high, high).astype(BF16)


def three_groups(v):
    v = jnp.where(lanes(v.shape) < G, v, 0.0)
    return jnp.concatenate([v + pltpu.roll(v, G, 1), v], axis=1)


def padded_first(weight, bias):
    shape = (8, weight.shape[1])
    extra = jnp.where(sublanes(shape) == 0, jnp.broadcast_to(bias, shape), 0.0)
    return jnp.concatenate([weight, extra], axis=0)


def store_packed(ref, layer, full):
    high, low = split(full)
    ref[layer, 0:G, :] = high
    ref[layer, G : 2 * G, :] = high
    ref[layer, 2 * G : 3 * G, :] = low
    ref[layer, 3 * G : W, :] = jnp.zeros_like(high)


def position():
    b = lax.axis_index("batch")
    return b & 1, (b >> 1) & 1, lax.axis_index("rep")


def noise_place(n):
    return slice(n // 4 * 8, n // 4 * 8 + 8), slice(n % 4 * 128, n % 4 * 128 + 128)


def forward_kernel(
    next_ref, act_ref, obs_ref, rew_ref, val_ref, len_ref, gain_ref, noise_ref, elite_ref,
    w1_ref, b1_ref, wm_ref, bm_ref, wo_ref, bo_ref,
    xs, xc_ref, cc_ref, pt_ref, count_ref, misc_ref, noise_out, hhs, hls, mhs, mls, pulls, *refs
):
    outs, (feat, wide, line, parts), splits, sems = refs[:5], refs[5:9], refs[9:14], refs[14]
    w1p, wmh, wml, woh, wol = splits
    copies = [pltpu.make_async_copy(a, b, sems.at[n]) for n, (a, b) in enumerate(zip(splits, outs))]
    horizon, latent, slots = next_ref.shape
    width = act_ref.shape[1]
    layers = w1_ref.shape[0]

    iterations, steps, samples, _ = noise_ref.shape
    elites = elite_ref.shape[2]
    base = lax.axis_index("batch") * samples
    line[...] = jnp.zeros_like(line)
    noise_out[...] = jnp.zeros_like(noise_out)
    square = (elites, elites)
    for i in range(iterations):
        chosen = jnp.broadcast_to(elite_ref[i], square)
        mine = jnp.max(jnp.where(lanes(square) == sublanes(square), chosen, -1), axis=1, keepdims=True)
        total = jnp.zeros((elites, 128), F32)
        for t in range(steps):
            line[0:samples, 0:width] = noise_ref[i, t]
            part = jnp.zeros((elites, 128), F32)
            for j in range(samples):
                row = jnp.broadcast_to(line[j : j + 1, :], (elites, 128))
                part = part + jnp.where(mine == base + j, row, 0.0)
            total = total + (pltpu.roll(part, t * width, 1) if t else part)
        for e in range(elites // 8):
            noise_out[noise_place(i * (elites // 8) + e)] = total[e * 8 : e * 8 + 8]

    wide[...] = jnp.zeros_like(wide)
    line[...] = jnp.zeros_like(line)
    for l in range(layers):
        store_packed(w1p, l, padded_first(w1_ref[l], b1_ref[l : l + 1, :]))
        wmh[l], wml[l] = split(wm_ref[l, 0])
        for g in range(3):
            wide[g * G : g * G + latent, :] = wo_ref[:, l, :]
        woh[l], wol[l] = split(wide[...].T)
    for copy in copies:
        copy.start()
    line[...] = jnp.zeros_like(line)
    line[0:1, 0:latent] = gain_ref[...]
    line[1 : 1 + layers, 0:latent] = bo_ref[...]
    small = three_groups(line[0:8, :])
    misc_ref[slots : slots + 8, :] = small

    def turned():
        v = feat[...].T
        return jnp.concatenate([v, jnp.where(lanes(v.shape) < G, v, 0.0)], axis=1)

    feat[...] = jnp.zeros_like(feat)
    for g in range(2):
        feat[g * G : g * G + latent, :] = obs_ref[...]
    obs = turned()
    misc_ref[0:slots, :] = obs
    for g in range(2):
        feat[g * G + ONE : g * G + ONE + 1, :] = jnp.ones((1, slots), F32)

    lengths = len_ref[...].astype(F32)
    before = jnp.where(sublanes((slots, slots)) < lanes((slots, slots)), 1.0, 0.0).astype(BF16)
    starts = dot(jnp.broadcast_to(lengths, (16, slots)).astype(BF16), before)[0:1]
    count = jnp.sum(lengths, axis=1, keepdims=True)
    count_ref[...] = jnp.broadcast_to(count, count_ref.shape)
    for g in range(2):
        feat[g * G + LENGTH : g * G + LENGTH + 1, :] = lengths
        feat[g * G + START : g * G + START + 1, :] = starts
    place = lanes((slots, pt_ref.shape[1]))

    lane = lanes((slots, W))
    part = lane % G
    is_latent = (part < latent) & (lane < 3 * G)
    is_target = (lane[:, 0:128] >= REWARD) & (lane[:, 0:128] <= COEF)
    is_input = (part >= latent) & (part <= ONE) & (lane < 3 * G)

    def step(t, carry):
        z, factor = carry
        coef = jnp.where(t < len_ref[...], factor, 0.0)
        for g in range(2):
            at = g * G
            feat[at : at + latent, :] = next_ref[t]
            feat[at + latent : at + latent + width, :] = act_ref[t]
            feat[at + REWARD : at + REWARD + 1, :] = rew_ref[pl.ds(t, 1), :]
            feat[at + VALUE : at + VALUE + 1, :] = val_ref[pl.ds(t, 1), :]
            feat[at + COEF : at + COEF + 1, :] = coef
        cond = turned()
        rows = pl.ds(pl.multiple_of(t * slots, slots), slots)
        live = t.astype(F32) < cond[:, LENGTH : LENGTH + 1]
        at = jnp.where(live, cond[:, START : START + 1] + t.astype(F32), -1.0).astype(jnp.int32)
        pt_ref[rows, :] = jnp.where(place == at, 1.0, 0.0).astype(BF16)
        rest = jnp.where(is_target, cond[:, 0:128], 0.0)
        packed = 0.0
        for n in range(3):
            high = rest.astype(BF16).astype(F32)
            rest = rest - high
            packed = packed + (pltpu.roll(high, 8 * n, 1) if n else high)
        parts[rows, :] = packed.astype(BF16)
        u = jnp.where(is_input, cond, 0.0)
        for l in range(layers):
            xp = pack_input(z + u)
            xs[l, rows, :] = xp
            high, low = split(elu(dot(xp, w1p[l])))
            hhs[l, rows, :] = high
            hls[l, rows, :] = low
            high, low = split(elu(dot_split(high, low, wmh[l], wml[l]) + bm_ref[l, 0:1, :]))
            mhs[l, rows, :] = high
            mls[l, rows, :] = low
            z = z + dot_split(high, low, woh[l], wol[l]) + small[1 + l : 2 + l, :]
        scale = (2.0 * consistency_coef / latent) * cond[:, COEF : COEF + 1]
        pulls[rows, :] = jnp.where(is_latent, scale * (z - cond), 0.0)
        return z, factor * rho_decay

    lax.fori_loop(0, horizon, step, (obs * small[0:1, :], jnp.float32(1.0 / (slots * horizon))))


    def gather(top, size):
        at = slice(top, top + size)
        found = dot_rows(pt_ref[:, at], jnp.concatenate([xs[l] for l in range(layers)] + [parts[...]], axis=1))
        for l in range(layers):
            xc_ref[l, at, :] = found[:, l * W : (l + 1) * W].astype(BF16)
        values = found[:, layers * W :]
        cc_ref[at, :] = values + (pltpu.roll(values, 120, 1) + pltpu.roll(values, 112, 1))

    gather(0, GATHERED)

    @pl.when(jnp.max(count) > SHORT)
    def _():
        gather(GATHERED, pt_ref.shape[1] - GATHERED)

    for copy in copies:
        copy.wait()


def send_halves(g, keep_ref, send_ref):
    core = lax.axis_index("rep")
    half = CHUNKS // 2
    keep_ref[...] = g[:, pl.ds(core * half, half)]
    send_ref[...] = g[:, pl.ds((1 - core) * half, half)]


def weight_grads(g, layer, xp, hh, hl, dph, dpl, doh, dol, extra):
    hidden = hh.shape[1]
    grad = dot_rows(hh, dph) + (dot_rows(hl, dph) + dot_rows(hh, dpl))
    rows = hidden // CHUNKS
    for c in range(CHUNKS):
        g[layer, c, 0:rows, :] = grad[c * rows : (c + 1) * rows]
    x = xp[:, 0 : 2 * G]
    both = dot_rows(x, doh) + dot_rows(x, dol)
    first = both[0:G] + both[G : 2 * G]
    for c in range(CHUNKS):
        part = first[c * 8 : c * 8 + 8]
        g[layer, c, rows : rows + 8, :] = part if c < CHUNKS - 1 else part + extra


def turn_weights(w1_ref, b1_ref, wm_ref, wo_ref, w1th, w1tl, wmth, wmtl, wotp, wide):
    latent = wo_ref.shape[0]
    wide[...] = jnp.zeros_like(wide)
    for l in range(w1_ref.shape[0]):
        full = padded_first(w1_ref[l], b1_ref[l : l + 1, :])
        turned = jnp.concatenate([full, full, full, jnp.zeros_like(full)], axis=0).T
        w1th[l], w1tl[l] = split(turned)
        wmth[l], wmtl[l] = split(wm_ref[l, 0].T)
        wide[0:latent, :] = wo_ref[:, l, :]
        store_packed(wotp, l, wide[...])


def heads_kernel(head, has_dx, turns, *refs):
    if turns:
        *refs, wide = refs
        dynamics = refs[11 + has_dx : 15 + has_dx]
        out = len(refs) - 16 - 5
        turn_weights(*dynamics, *refs[out : out + 5], wide)
        refs = refs[:out] + refs[out + 5 :]

    (xp_ref, cond_ref, count_ref, w1_ref, b1_ref, wm_ref, bm_ref, ng_ref, nb_ref, p_ref, sb_ref) = refs[:11]
    refs = refs[11:]
    dx_in = refs[0] if has_dx else None
    refs = refs[1:] if has_dx else refs
    (
        keep_ref, send_ref, dx_ref, w1_out, wmh_out, wml_out,
        w1p, wmh, wml, w1th, w1tl, wmth, wmtl, hh, hl, dph, dpl, doh, dol, sums, g, sems,
    ) = refs[len(refs) - 22 :]
    layers = xp_ref.shape[0]
    capacity = hh.shape[1]
    short = jnp.max(count_ref[...]) <= SHORT
    blocks = jnp.where(short, SHORT // ROW_BLOCK, capacity // ROW_BLOCK)
    for l in range(layers):
        dx_ref[l, SHORT:, :] = jnp.zeros((dx_ref.shape[1] - SHORT, W), F32)
    is_reward = head == 1
    target_lane = REWARD if is_reward else VALUE
    scale = 2.0 * (reward_coef if is_reward else value_coef)
    for l in range(layers):
        full = padded_first(w1_ref[l], b1_ref[l : l + 1, :])
        store_packed(w1p, l, full)
        turned = jnp.concatenate([full, full, full, jnp.zeros_like(full)], axis=0).T
        w1th[l], w1tl[l] = split(turned)
        wm = wm_ref[l, 0]
        wmh[l], wml[l] = split(wm)
        wmth[l], wmtl[l] = split(wm.T)
    weights = [
        pltpu.make_async_copy(src, dst, sems.at[n])
        for n, (src, dst) in enumerate(((w1p, w1_out), (wmh, wmh_out), (wml, wml_out)))
    ]
    for copy in weights:
        copy.start()
    sums[...] = jnp.zeros_like(sums)

    def block(i, carry):
        rows = pl.ds(pl.multiple_of(i * ROW_BLOCK, ROW_BLOCK), ROW_BLOCK)
        kept = []
        score = 0.0
        for l in range(layers):
            o = dot(xp_ref[l, rows, :], w1p[l])
            if is_reward:
                h = elu(o)
                norm = None
            else:
                centered = o - jnp.mean(o, axis=-1, keepdims=True)
                variance = jnp.mean(centered * centered, axis=-1, keepdims=True)
                scale_rows = lax.rsqrt(variance + norm_epsilon)
                unit = centered * scale_rows
                gain = ng_ref[l, head - 2 : head - 1, :]
                h = jnp.tanh(unit * gain + nb_ref[l, head - 2 : head - 1, :])
                norm = (unit, scale_rows, gain)
            high, low = split(h)
            hh[l, rows, :] = high
            hl[l, rows, :] = low
            m = elu(dot_split(high, low, wmh[l], wml[l]) + bm_ref[l, head : head + 1, :])
            p = p_ref[head - 1, l : l + 1, :]
            score = score + jnp.sum(m * p, axis=-1, keepdims=True) + sb_ref[l, head - 1]
            kept.append((h, norm, m, p))
        cond = cond_ref[rows, :]
        miss = score - cond[:, target_lane : target_lane + 1]
        dscore = (scale * cond[:, COEF : COEF + 1]) * miss
        dscore_sum = jnp.sum(dscore, axis=0, keepdims=True)
        for l in range(layers):
            h, norm, m, p = kept[l]
            dp = jnp.sum(dscore * m, axis=0, keepdims=True)
            dpre = (dscore * p) * elu_slope(m)
            dbm = jnp.sum(dpre, axis=0, keepdims=True)
            high, low = split(dpre)
            dph[l, rows, :] = high
            dpl[l, rows, :] = low
            dh = dot_split(high, low, wmth[l], wmtl[l])
            if is_reward:
                do = dh * elu_slope(h)
            else:
                unit, scale_rows, gain = norm
                dn = dh * (1.0 - h * h)
                sums[l, 2:3, :] += jnp.sum(dn * unit, axis=0, keepdims=True)
                sums[l, 3:4, :] += jnp.sum(dn, axis=0, keepdims=True)
                dunit = dn * gain
                do = scale_rows * (
                    dunit
                    - jnp.mean(dunit, axis=-1, keepdims=True)
                    - unit * jnp.mean(dunit * unit, axis=-1, keepdims=True)
                )
            sums[l, 1:2, :] += dbm
            sums[l, 4:5, :] += dp
            sums[l, 5:6, :] += jnp.broadcast_to(dscore_sum, (1, sums.shape[2]))
            high, low = split(do)
            doh[l, rows, :] = high
            dol[l, rows, :] = low
            dx = dot_split(high, low, w1th[l], w1tl[l])
            dx_ref[l, rows, :] = dx_in[l, rows, :] + dx if has_dx else dx
        return carry

    lax.fori_loop(0, blocks, block, 0)

    def finish(n):
        for l in range(layers):
            rows = [ref[l, 0:n, :] for ref in (hh, hl, dph, dpl, doh, dol)]
            weight_grads(g, l, xp_ref[l, 0:n, :], *rows, sums[l])

    pl.when(short)(functools.partial(finish, SHORT))
    pl.when(jnp.logical_not(short))(functools.partial(finish, capacity))
    send_halves(g, keep_ref, send_ref)
    for copy in weights:
        copy.wait()


def backward_kernel(
    xp_ref, hh_ref, hl_ref, mh_ref, ml_ref, pull_ref, dx_ref, misc_ref,
    w1th, w1tl, wmth, wmtl, wotp, pt_ref, count_ref, *rest
):
    keep_ref, send_ref, dobs_ref, dxs, dph, dpl, doh, dol, dzs, sums, g = rest[len(rest) - 11 :]
    layers, rows_all = xp_ref.shape[0], xp_ref.shape[1]
    latent, slots = dobs_ref.shape
    horizon = rows_all // slots
    hidden = wmth.shape[-1]
    sums[...] = jnp.zeros_like(sums)

    def scatter(n):
        parts = [split(dx_ref[l, 0:n, :]) for l in range(layers)]
        found = dot(pt_ref[:, 0:n], jnp.concatenate([v for pair in parts for v in pair], axis=1))
        for l in range(layers):
            at = 2 * l * W
            dxs[l] = found[:, at : at + W] + found[:, at + W : at + 2 * W]

    short = jnp.max(count_ref[...]) <= SHORT
    pl.when(short)(functools.partial(scatter, GATHERED))
    pl.when(jnp.logical_not(short))(functools.partial(scatter, pt_ref.shape[1]))
    lane = lanes((slots, W))
    is_latent = ((lane % G) < latent) & (lane < 3 * G)

    def step(i, dz):
        t = horizon - 1 - i
        rows = pl.ds(pl.multiple_of(t * slots, slots), slots)
        dz = dz + pull_ref[rows, :]
        for l in reversed(range(layers)):
            dzp = pack_input(dz)
            dzs[l, rows, :] = dzp[:, 0 : 2 * G]
            sums[l, 2:3, 0:W] += jnp.sum(dz, axis=0, keepdims=True)
            m = mh_ref[l, rows, :].astype(F32) + ml_ref[l, rows, :].astype(F32)
            dpre = dot(dzp, wotp[l]) * elu_slope(m)
            sums[l, 1:2, :] += jnp.sum(dpre, axis=0, keepdims=True)
            high, low = split(dpre)
            dph[l, rows, :] = high
            dpl[l, rows, :] = low
            h = hh_ref[l, rows, :].astype(F32) + hl_ref[l, rows, :].astype(F32)
            do = dot_split(high, low, wmth[l], wmtl[l]) * elu_slope(h)
            high, low = split(do)
            doh[l, rows, :] = high
            dol[l, rows, :] = low
            dx = dot_split(high, low, w1th[l], w1tl[l]) + dxs[l, rows, :]
            dz = dz + jnp.where(is_latent, dx, 0.0)
        return dz

    dz = lax.fori_loop(0, horizon, step, jnp.zeros((slots, W), F32))
    dobs_ref[...] = (dz * misc_ref[slots : slots + 1, :])[:, 0:128].T[0:latent]
    sums[0, 3:4, 0:W] = jnp.sum(dz * misc_ref[0:slots, :], axis=0, keepdims=True)
    rows = hidden // CHUNKS
    for l in range(layers):
        weight_grads(g, l, xp_ref.at[l], hh_ref[l], hl_ref[l], dph[l], dpl[l], doh[l], dol[l], sums[l])
        both = dot_rows(dzs[l], mh_ref[l]) + dot_rows(dzs[l], ml_ref[l])
        out = both[0:G] + both[G : 2 * G]
        for c in range(CHUNKS):
            g[l, c, rows + 8 : rows + 16, :] = out[c * 8 : c * 8 + 8]
    send_halves(g, keep_ref, send_ref)


def planner_kernel(iterations, first, *refs):
    weights = refs[:14]
    state_in = refs[14:17] if first else refs[14:15]
    refs = refs[17:] if first else refs[15:]
    (noise_ref, misc_ref, bm_ref, ng_ref, nb_ref, p_ref, sb_ref) = refs[:7]
    out_ref, xs, acts, line = refs[len(refs) - 4 :]
    w1p, wmh, wml = weights[0:4], weights[4:8], weights[8:12]
    woh, wol = weights[12:14]
    horizon, elites = acts.shape[0], acts.shape[1]
    layers = w1p[0].shape[0]
    slots = misc_ref.shape[0] - 8
    latent = 50

    lane = lanes((1, W))
    is_action = ((lane % G) >= latent) & ((lane % G) < ONE) & (lane < 3 * G)
    is_one = ((lane % G) == ONE) & (lane < 3 * G)
    group = lane // G

    def placed(v, at):
        return jnp.where(is_action, three_groups(pltpu.roll(v, (latent - at) % 128, 1)), 0.0)

    def three(v):
        high = v.astype(BF16)
        rest = v - high.astype(F32)
        mid = rest.astype(BF16)
        return high, mid, (rest - mid.astype(F32)).astype(BF16)

    def dot_fine(v, w_high, w_low):
        n = v.shape[0]
        high, mid, low = three(v)
        a = dot(jnp.concatenate([high, mid, low], axis=0), w_high)
        b = dot(jnp.concatenate([high, mid], axis=0), w_low)
        return a[0:n] + (a[n : 2 * n] + b[0:n] + (a[2 * n : 3 * n] + b[n : 2 * n]))

    def dot_first(x, w):
        n = x.shape[0]
        high, mid, low = three(x)
        keep = (group == 0) | (group == 2)
        zero = jnp.zeros_like(high)
        high = jnp.where(keep, high, zero)
        mid = jnp.where(keep, mid, zero)
        low = jnp.where(group == 0, low, zero)
        a = dot(jnp.concatenate([high, mid, low], axis=0), w)
        return a[0:n] + (a[n : 2 * n] + a[2 * n : 3 * n])

    def middle(h, l, k):
        return elu(dot_fine(h, wmh[k][l], wml[k][l]) + bm_ref[l, k : k + 1, :])

    def head(m, l, k):
        return jnp.sum(m * p_ref[k - 1, l : l + 1, :], axis=-1, keepdims=True) + sb_ref[l, k - 1]

    def value(x, l, k):
        o = dot_first(x, w1p[k][l])
        centered = o - jnp.mean(o, axis=-1, keepdims=True)
        variance = jnp.mean(centered * centered, axis=-1, keepdims=True)
        unit = centered * lax.rsqrt(variance + norm_epsilon)
        h = jnp.tanh(unit * ng_ref[l, k - 2 : k - 1, :] + nb_ref[l, k - 2 : k - 1, :])
        return head(middle(h, l, k), l, k)

    if first:
        mean_ref, std_ref, start_ref = state_in
        line[...] = jnp.zeros_like(line)
        line[0:horizon, 0:6] = mean_ref[...]
        line[8 : 8 + horizon, 0:6] = std_ref[...]
        line[16:17, 0:latent] = start_ref[...]
        for t in range(horizon):
            out_ref[0, t : t + 1, :] = placed(line[t : t + 1, :], 0)
            out_ref[1, t : t + 1, :] = placed(line[8 + t : 9 + t, :], 0)
        out_ref[2, 0:1, :] = three_groups(line[16:17, :])
        state_ref = out_ref
    else:
        (state_ref,) = state_in
        out_ref[2] = state_ref[2]

    start = state_ref[2, 0:1, :]
    for iteration in iterations:
        tiles = elites // 8
        noise = [noise_ref[noise_place(iteration * tiles + e)] for e in range(tiles)]
        noise = jnp.concatenate(noise, axis=0) if tiles > 1 else noise[0]
        for t in range(horizon):
            acts[t] = jnp.where(
                is_action,
                jnp.tanh(state_ref[0, t : t + 1, :] + state_ref[1, t : t + 1, :] * placed(noise, 6 * t)),
                0.0,
            )
        z = jnp.broadcast_to(start, (elites, W))
        for t in range(horizon):
            u = jnp.where(is_one, 1.0, acts[t])
            for l in range(layers):
                x = z + u
                xs[l, t] = x
                if t < horizon - 1 or l < layers - 1:
                    m = middle(elu(dot_first(x, w1p[0][l])), l, 0)
                    z = z + dot_fine(m, woh[l], wol[l]) + misc_ref[slots + 1 + l : slots + 2 + l, :]
        reward = 0.0
        one = 0.0
        two = 0.0
        for l in range(layers):
            x = xs[l].reshape(horizon * elites, W)
            reward = reward + head(middle(elu(dot_first(x, w1p[1][l])), l, 1), l, 1)
            x = xs[l, horizon - 1]
            one = one + value(x, l, 2)
            two = two + value(x, l, 3)
        returns = discount ** (horizon - 1) * jnp.minimum(one, two)
        for t in range(horizon):
            returns = returns + discount**t * reward[t * elites : (t + 1) * elites]
        top = jnp.max(returns, axis=0, keepdims=True)
        weight = jnp.exp(exponent_sharpness_level * (returns - top))
        total = jnp.sum(weight, axis=0, keepdims=True)
        for t in range(horizon):
            sampled = acts[t]
            mean = jnp.sum(weight * sampled, axis=0, keepdims=True) / total
            centered = sampled - mean
            variance = jnp.sum(weight * (centered * centered), axis=0, keepdims=True) / total
            out_ref[0, t : t + 1, :] = mean
            out_ref[1, t : t + 1, :] = jnp.sqrt(variance + std_floor * std_floor)
        state_ref = out_ref


CORE = 0


def bits():
    x, y, _ = position()
    return ((x, y, lambda f, s: f + 2 * s), (y, x, lambda f, s: 2 * f + s))


def first_partner(l):
    return (1, 2)[l]


def second_partner(l):
    return (2, 1)[l]


def blocks(ref, rows):
    def at(n):
        return ref.at[pl.ds(n * rows, rows)]

    return at


def add_first(rows, ins, keeps, sends):
    keep, recv = (blocks(r, rows) for r in ins)
    kept = blocks(keeps[0], rows)
    for l, (f, _, chunk) in enumerate(bits()):
        sent = blocks(sends[l], rows)
        for m in range(2):
            mine, other = 4 * l + chunk(f, m), 4 * l + chunk(1 - f, m)
            kept(2 * l + m)[...] = keep(mine)[...] + recv(mine)[...]
            sent(m)[...] = keep(other)[...] + recv(other)[...]


def add_second(rows, ins, keeps, sends):
    keep, kept = blocks(ins[0], rows), blocks(keeps[0], rows)
    for l, (_, s, _) in enumerate(bits()):
        recv = blocks(ins[1 + l], rows)
        kept(l)[...] = keep(2 * l + s)[...] + recv(s)[...]
        sends[l][...] = keep(2 * l + 1 - s)[...] + recv(1 - s)[...]


def add_third(rows, ins, keeps, sends):
    for l in range(2):
        at = slice(l * rows, l * rows + rows)
        total = ins[0][at] + ins[1 + l][...]
        for ref in (*keeps, *sends):
            ref[at] = total


def add_whole(rows, ins, keeps, sends):
    total = ins[0][...]
    for ref in ins[1:]:
        total = total + ref[...]
    for ref in (*keeps, *sends):
        ref[...] = total


def add_last(rows, ins, keeps, sends):
    total = ins[0][...] + ins[1][...]
    keeps[0][...] = total
    for l in range(2):
        sends[l][...] = total[l * rows : l * rows + rows]


def join_two(rows, ins, keeps, sends):
    kept = blocks(keeps[0], rows)
    for l, (_, s, _) in enumerate(bits()):
        own, sent = ins[0][l * rows : l * rows + rows], blocks(sends[l], rows)
        recv = ins[1 + l][...]
        for at, value in ((s, own), (1 - s, recv)):
            kept(2 * l + at)[...] = value
            sent(at)[...] = value


def join_four(rows, ins, keeps, sends):
    own = blocks(ins[0], rows)
    for l, (f, _, chunk) in enumerate(bits()):
        recv = blocks(ins[1 + l], rows)
        for m in range(2):
            for at, value in ((chunk(f, m), own(2 * l + m)[...]), (chunk(1 - f, m), recv(m)[...])):
                for ref in (*keeps, *sends):
                    blocks(ref, rows)(4 * l + at)[...] = value


class Received:
    def __init__(self, buffer, start, rows):
        self.buffer, self.start, self.rows = buffer, start, rows


class Sums:
    def __init__(self, batch):
        self.batch = batch
        self.pending = []
        self.after = []
        self.late = []

    def swap(self, a, partner):
        if partner == CORE:
            return lax.ppermute(a, "rep", [(0, 1), (1, 0)])
        return lax.ppermute(a, "batch", [(i, i ^ partner) for i in range(self.batch)])

    def start(self, steps, done):
        self.pending.append([steps, done, next(steps)])

    def advance(self):
        if not self.pending:
            return
        jobs = [entry[2] for entry in self.pending]
        arrays, buffers = [], {}
        for _, _, ins, _, sends in jobs:
            for a in ins:
                a = a.buffer if isinstance(a, Received) else a
                if not any(a is b for b in arrays):
                    arrays.append(a)
            for partner, rows in sends:
                buffers[partner] = buffers.get(partner, 0) + rows
        partners = list(buffers)
        width = jobs[0][2][0].shape[-1]
        out_shape = [f32((n, width)) for _, _, _, keeps, _ in jobs for n in keeps]
        out_shape += [f32((buffers[p], width)) for p in partners] + [f32((8, 128))]
        after = self.after + self.late

        def kernel(*refs):
            ins_all, outs = refs[: len(arrays)], list(refs[len(arrays) + len(after) :])
            outs.pop()[...] = jnp.zeros((8, 128), F32)
            sent_refs = dict(zip(partners, outs[len(outs) - len(partners) :]))
            used = dict.fromkeys(partners, 0)
            for fn, rows, ins, keeps, sends in jobs:
                in_refs = []
                for a in ins:
                    whole = a.buffer if isinstance(a, Received) else a
                    ref = ins_all[[whole is b for b in arrays].index(True)]
                    in_refs.append(ref.at[pl.ds(a.start, a.rows)] if isinstance(a, Received) else ref)
                sent = []
                for partner, n in sends:
                    sent.append(sent_refs[partner].at[pl.ds(used[partner], n)])
                    used[partner] += n
                fn(rows, in_refs, outs[: len(keeps)], sent)
                outs = outs[len(keeps) :]

        outs = pl.pallas_call(
            kernel,
            in_specs=[vmem()] * len(arrays) + [hbm()] * len(after),
            out_specs=[vmem()] * len(out_shape),
            out_shape=out_shape,
            compiler_params=params(20),
            cost_estimate=cost(6),
            name="add_up",
        )(*arrays, *after)
        token = outs[-1]
        received = {p: self.swap(a, p) for p, a in zip(partners, outs[len(outs) - 1 - len(partners) :])}
        used = dict.fromkeys(partners, 0)
        self.late = []
        for entry, (_, _, _, keeps, sends) in zip(list(self.pending), jobs):
            result = list(outs[: len(keeps)])
            outs = outs[len(keeps) :]
            for partner, n in sends:
                result.append(Received(received[partner], used[partner], n))
                used[partner] += n
            try:
                entry[2] = entry[0].send(result)
            except StopIteration as stop:
                self.pending.remove(entry)
                entry[1].append(stop.value)
                if isinstance(stop.value[-1], Received):
                    self.late.append(stop.value[-1].buffer)
        self.after = [token]

    def sum_small(self, a):
        rows, bit, steps = a.shape[0], 8, []
        while bit < self.batch:
            steps.append(bit)
            bit *= 2
        steps += [1, 2, 4][: 3 if self.batch > 4 else 2]
        recv = self.swap(a, steps[0])
        for partner in steps[1:]:
            a, recv = yield (add_whole, rows, (a, recv), (rows,), ((partner, rows),))
        (a,) = yield (add_whole, rows, (a, recv), (rows,), ())
        return (a,)

    def sum_batch(self, keep, send):
        _, _, rows, hidden = keep.shape
        keep, send = keep.reshape(-1, hidden), send.reshape(-1, hidden)
        to_first = tuple((first_partner(l), 2 * rows) for l in range(2))
        to_second = tuple((second_partner(l), rows) for l in range(2))
        keep, ra, rb = yield (add_first, rows, (keep, self.swap(send, CORE)), (4 * rows,), to_first)
        keep, ra, rb = yield (add_second, rows, (keep, ra, rb), (2 * rows,), to_second)
        keep, recv = yield (add_third, rows, (keep, ra, rb), (2 * rows,), ((4, 2 * rows),))
        bit = 8
        while bit < self.batch:
            keep, recv = yield (add_whole, rows, (keep, recv), (2 * rows,), ((bit, 2 * rows),))
            bit *= 2
        keep, ra, rb = yield (add_last, rows, (keep, recv), (2 * rows,), to_second)
        keep, ra, rb = yield (join_two, rows, (keep, ra, rb), (4 * rows,), to_first)
        keep, recv = yield (join_four, rows, (keep, ra, rb), (8 * rows,), ((CORE, 8 * rows),))
        return rows, keep, recv


def vmem():
    return pl.BlockSpec(memory_space=pltpu.VMEM)


def smem():
    return pl.BlockSpec(memory_space=pltpu.SMEM)


def hbm():
    return pl.BlockSpec(memory_space=pl.ANY)


def params(mebibytes):
    return pltpu.CompilerParams(vmem_limit_bytes=mebibytes * 1024 * 1024)


def in_hbm(a):
    return pltpu.with_memory_space_constraint(a, pltpu.HBM)


def cost(us):
    return pl.CostEstimate(flops=int(us * 1e9), bytes_accessed=0, transcendentals=0)


def shape_of(a):
    return jax.ShapeDtypeStruct(a.shape, a.dtype)


def assemble_kernel(hidden, latent, batches, *refs):
    half = CHUNKS // 2
    parts, heights = {}, {}
    for n, (k, height, start) in enumerate(batches):
        parts[k] = [refs[2 * n], refs[2 * n + 1].at[pl.ds(start, height * CHUNKS)]]
        heights[k] = height
    last = 0 in parts
    core = lax.axis_index("rep")
    rows = hidden // CHUNKS
    copies = []
    if last:
        small_in, dobs_in = refs[2 * len(batches) + 2 : 2 * len(batches) + 4]
        (
            mid_ref, first_ref, bias_ref, mid_bias_ref, ng_ref, nb_ref, wo_ref, bo_ref, p_ref, sb_ref, gain_ref,
            dobs_ref, sems,
        ) = refs[len(refs) - 13 :]
        dobs_ref[...] = dobs_in[...]
    else:
        mid_ref, first_ref, small_ref, sems = refs[len(refs) - 4 :]

    def copy(src, dst, sem, when=None):
        made = pltpu.make_async_copy(src, dst, sem)
        if when is None:
            made.start()
        else:
            pl.when(when)(made.start)
        return made

    for k in parts:
        at = pl.ds(k * hidden, hidden)
        for l in range(2):
            for m, owner in ((0, core), (1, 1 - core)):
                for j in range(half):
                    top = (l * half + j) * heights[k]
                    src = parts[k][m].at[pl.ds(top, rows)]
                    copies.append(copy(src, mid_ref.at[l, k, owner * half + j], sems.at[0, k, l, m, j]))
                    rest = parts[k][m].at[pl.ds(top + rows, 8)]
                    lower = copy(rest, first_ref.at[l, j, :, at], sems.at[1, k, l, 0, j], owner == 0)
                    if m == 0:
                        copies.append(lower)
                    if j < half - 1:
                        upper = copy(rest, first_ref.at[l, half + j, :, at], sems.at[1, k, l, 1, j], owner == 1)
                        if m == 0:
                            copies.append(upper)

    def chunk(k, l, c, lo, hi):
        top = (l * half + c % half) * heights[k] + rows
        own, other = (parts[k][m][top + lo : top + hi, :] for m in range(2))
        return jnp.where(core == c // half, own, other)

    if last:
        for l in range(2):
            for k in range(4):
                small = chunk(k, l, CHUNKS - 1, 0, 8) if k in parts else small_in[k, l]
                bias_ref[l : l + 1, k * hidden : (k + 1) * hidden] = small[0:1]
                mid_bias_ref[l, k : k + 1, :] = small[1:2]
                if k >= 1:
                    p_ref[k - 1, l : l + 1, :] = small[4:5]
                    sb_ref[l : l + 1, k - 1 : k] = small[5:6, 0:1]
                if k >= 2:
                    ng_ref[l, k - 2 : k - 1, :] = small[2:3]
                    nb_ref[l, k - 2 : k - 1, :] = small[3:4]
                if k == 0:
                    bo_ref[l : l + 1, :] = small[2:3, 0:latent]
                    if l == 0:
                        gain_ref[...] = small[3:4, 0:latent]
            for c in range(CHUNKS - 1):
                n = min(8, latent - 8 * c)
                wo_ref[8 * c : 8 * c + n, l, :] = chunk(0, l, c, 8, 8 + n)
    else:
        small_ref[...] = jnp.zeros_like(small_ref)
        for k in parts:
            for l in range(2):
                small_ref[k, l] = chunk(k, l, CHUNKS - 1, 0, 8)
    for made in copies:
        made.wait()


def shards(
    obs_latent, actions, next_latent, reward_target, value_target, lengths,
    first_weight, opening_layer_offset, mid_weight, mid_bias, norm_gain, norm_bias,
    latent_out, latent_bias, payoff_critic_projection, scalar_bias, obs_gain,
    plan_start, action_guess_average, plan_init_std, action_noise, elite_index,
    *, batch,
):
    slots, latent = obs_latent.shape
    horizon, width = actions.shape[1], actions.shape[2]
    layers, hidden = first_weight.shape[0], mid_weight.shape[-1]
    rows_all = slots * horizon
    joint = latent + width
    iterations, samples_local, plan_horizon = action_noise.shape[1:4]
    elites = elite_index.shape[-1]
    heads = 3
    sums = Sums(batch)

    projection = jnp.transpose(payoff_critic_projection, (1, 0, 2))
    wout = jnp.transpose(latent_out, (2, 0, 1))

    def column(k):
        return [
            pl.BlockSpec((layers, joint, hidden), lambda i: (0, 0, k)),
            pl.BlockSpec((layers, hidden), lambda i: (0, k)),
            pl.BlockSpec((layers, 1, hidden, hidden), lambda i: (0, k, 0, 0)),
        ]

    def scratch(*shape, dtype=BF16):
        return pltpu.VMEM(shape, dtype)

    def copies(*shapes):
        return [scratch(*v.shape, dtype=v.dtype) for v in shapes]

    def to_hbm(*shapes):
        return [pltpu.HBM(v.shape, v.dtype) for v in shapes]

    def weights_of(*arrays):
        return [in_hbm(a) for a in arrays]

    square = bf((layers, hidden, hidden))
    narrow = bf((layers, hidden, W))
    packed = bf((layers, W, hidden))
    wide_rows = bf((layers, rows_all, hidden))
    noise_shape = f32((8 * -(-iterations * (elites // 8) // 4), hidden))
    kept = [packed, square, square, narrow, narrow]
    capacity = -(-rows_all // ROW_BLOCK) * ROW_BLOCK
    gathered = -(-capacity // 128) * 128
    (xp, xc, cc, pt, live_count, misc, noise, hh, hl, mh, ml, pull, w1p, wmh, wml, woh, wol) = pl.pallas_call(
        forward_kernel,
        grid=(1,),
        in_specs=[vmem()] * 9 + column(0) + [vmem()] * 3,
        out_specs=[vmem()] * 12 + [hbm()] * 5,
        out_shape=[
            bf((layers, rows_all, W)), bf((layers, gathered, W)), f32((gathered, 128)), bf((rows_all, gathered)),
            f32((8, 128)), f32((slots + 8, W)), noise_shape,
            *[wide_rows] * 4, f32((rows_all, W)), *to_hbm(*kept),
        ],
        scratch_shapes=[
            scratch(2 * G, slots, dtype=F32),
            scratch(W, hidden, dtype=F32),
            scratch(max(8, samples_local), 128, dtype=F32),
            scratch(rows_all, 128),
            *copies(*kept),
            pltpu.SemaphoreType.DMA((5,)),
        ],
        compiler_params=params(26),
        cost_estimate=cost(20),
        name="forward_chain",
    )(
        *weights_of(
            jnp.transpose(next_latent, (1, 2, 0)), jnp.transpose(actions, (1, 2, 0)), obs_latent.T,
            reward_target.T, value_target.T, lengths[None], obs_gain[None],
            jnp.transpose(action_noise[0], (0, 2, 1, 3)), jnp.transpose(elite_index, (1, 0, 2)),
            first_weight, opening_layer_offset, mid_weight, mid_bias, wout, latent_bias,
        )
    )
    noise_done = []
    split_weights = [(w1p, wmh, wml)]

    summed = [[] for _ in range(4)]
    dx = None
    rows = hidden // CHUNKS + 8
    half = f32((layers, CHUNKS // 2, rows, hidden))
    for head in range(1, 1 + heads):
        has_dx = dx is not None
        turns = head == heads
        keep, send, dx, *weights = pl.pallas_call(
            functools.partial(heads_kernel, head, has_dx, turns),
            grid=(1,),
            in_specs=[vmem()] * 3 + column(head) + [vmem()] * 4 + [smem()] + [vmem()] * has_dx
            + (column(0) + [vmem()] if turns else []) + [hbm()] * len(sums.after),
            out_specs=[vmem()] * 3 + [hbm()] * 3 + [vmem()] * (5 * turns),
            out_shape=[half, half, f32((layers, gathered, W)), *to_hbm(packed, square, square)]
            + [narrow, narrow, square, square, packed] * turns,
            scratch_shapes=[
                *copies(packed, square, square, narrow, narrow, square, square),
                *[scratch(layers, capacity, hidden)] * 6,
                scratch(layers, 8, hidden, dtype=F32),
                scratch(layers, CHUNKS, rows, hidden, dtype=F32),
                pltpu.SemaphoreType.DMA((3,)),
                *[scratch(G, hidden, dtype=F32)] * turns,
            ],
            compiler_params=params(HEAD_LIMIT),
            cost_estimate=cost(15),
            name=f"head_{head}",
        )(
            xc, cc, live_count,
            *weights_of(
                first_weight, opening_layer_offset, mid_weight, mid_bias,
                norm_gain, norm_bias, projection, scalar_bias,
            ),
            *([dx] if has_dx else []),
            *(weights_of(first_weight, opening_layer_offset, mid_weight, wout) if turns else []), *sums.after,
        )
        split_weights.append(tuple(weights[:3]))
        turned = weights[3:]
        sums.after = [dx]
        sums.advance()
        sums.start(sums.sum_batch(keep, send), summed[head])
        if head == 1:
            sums.start(sums.sum_small(noise), noise_done)

    rows = hidden // CHUNKS + 16
    half = f32((layers, CHUNKS // 2, rows, hidden))
    keep, send, dobs = pl.pallas_call(
        backward_kernel,
        grid=(1,),
        in_specs=[vmem()] * 15 + [hbm()] * len(sums.after),
        out_specs=[vmem()] * 3,
        out_shape=[half, half, f32((latent, slots))],
        scratch_shapes=[
            scratch(layers, rows_all, W, dtype=F32),
            *[scratch(layers, rows_all, hidden)] * 4,
            scratch(layers, rows_all, 2 * G),
            scratch(layers, 8, hidden, dtype=F32),
            scratch(layers, CHUNKS, rows, hidden, dtype=F32),
        ],
        compiler_params=params(BACK_LIMIT),
        cost_estimate=cost(25),
        name="backward_chain",
    )(xp, hh, hl, mh, ml, pull, dx, misc, *turned, pt, live_count, *sums.after)
    sums.after = [dobs]
    sums.advance()
    sums.start(sums.sum_batch(keep, send), summed[0])

    while not noise_done:
        sums.advance()
    ((noise,),) = noise_done
    flat_weights = [w[n] for n in range(3) for w in split_weights] + [woh, wol]
    state = [action_guess_average[0], plan_init_std[0], plan_start]
    groups = [[i] for i in range(iterations)]
    if iterations > 5:
        groups[3:5] = [groups[3] + groups[4]]
    for group in groups:
        i = group[0]
        state = [
            pl.pallas_call(
                functools.partial(planner_kernel, group, i == 0),
                in_specs=[vmem()] * (14 + len(state)) + [vmem()] * 6 + [smem()]
                + [hbm()] * len(sums.after),
                out_specs=vmem(),
                out_shape=f32((3, plan_horizon, W)),
                scratch_shapes=[
                    scratch(layers, plan_horizon, elites, W, dtype=F32),
                    scratch(plan_horizon, elites, W, dtype=F32),
                    scratch(24, 128, dtype=F32),
                ],
                compiler_params=params(20),
                cost_estimate=cost(9 * len(group)),
                name=f"planner_{i}",
            )(
                *flat_weights, *state, noise, misc, mid_bias, norm_gain, norm_bias, projection,
                scalar_bias, *sums.after,
            )
        ]
        sums.after = [state[0]]
        sums.advance()
    plan = state[0][:2, None, :, latent:joint]
    big = [
        f32((layers, 4, CHUNKS, hidden // CHUNKS, hidden)), f32((layers, CHUNKS - 1, 8, 4 * hidden)),
    ]

    def assemble(heads_done, more, out_shape, aliases, name, after):
        done = [(k, *summed[k][0]) for k in heads_done]
        pieces = [p for _, _, own, other in done for p in (own, other.buffer)]
        spec = tuple((k, rows, other.start) for k, rows, _, other in done)
        return pl.pallas_call(
            functools.partial(assemble_kernel, hidden, latent, spec),
            in_specs=[vmem()] * len(pieces) + [hbm(), hbm(), vmem(), vmem()][: len(more)] + [hbm()] * len(after),
            out_specs=[hbm(), hbm()] + [vmem()] * (len(out_shape) - 2),
            out_shape=out_shape,
            scratch_shapes=[pltpu.SemaphoreType.DMA((2, 4, 2, 2, CHUNKS // 2))],
            input_output_aliases={len(pieces) + n: n for n in range(2)} if aliases else {},
            compiler_params=params(24),
            cost_estimate=cost(3),
            name=name,
        )(*pieces, *more, *after)

    early = [k for k in range(4) if summed[k]]
    held = assemble(early, [], big + [f32((4, layers, 8, hidden))], False, "assemble_early", sums.after)
    sums.after = [held[2]]
    while sums.pending:
        sums.advance()
    late = [k for k in range(4) if k not in early]
    mids, firsts, *outs = assemble(
        late,
        [*held, dobs],
        big
        + [
            f32(opening_layer_offset.shape), f32(mid_bias.shape), f32(norm_gain.shape), f32(norm_bias.shape),
            f32(wout.shape), f32(latent_bias.shape), f32(projection.shape), f32(scalar_bias.shape), f32((1, latent)),
            f32(dobs.shape),
        ],
        True,
        "assemble",
        sums.after,
    )
    return (
        firsts.reshape(first_weight.shape),
        outs[0],
        mids.reshape(mid_weight.shape),
        *outs[1:4],
        jnp.transpose(outs[4], (1, 2, 0)),
        outs[5],
        jnp.transpose(outs[6], (1, 0, 2)),
        outs[7],
        outs[8][0],
        outs[9].T,
        plan[0],
        plan[1],
    )


def solution(mesh):
    rows = ("batch", "rep")
    return jax.shard_map(
        functools.partial(shards, batch=mesh.shape["batch"]),
        mesh=mesh,
        in_specs=(
            P(rows, None), P(rows, None, None), P(rows, None, None), P(rows, None), P(rows, None), P(rows),
            P(), P(), P(), P(), P(), P(), P(), P(), P(), P(), P(),
            P("rep", None), P("rep", None, None), P("rep", None, None),
            P("rep", None, "batch", None, None), P("rep", None, None),
        ),
        out_specs=(P(),) * 11 + (P(rows, None), P("rep", None, None), P("rep", None, None)),
        check_vma=False,
    )
```

```python
import functools

import jax
import jax.numpy as jnp
from jax import lax
from jax.experimental import pallas as pl
from jax.experimental.pallas import tpu as pltpu
from jax.sharding import PartitionSpec as P

F32 = jnp.float32
BF16 = jnp.bfloat16

rho_decay = 0.5
consistency_coef = 2.0
reward_coef = 0.5
value_coef = 0.1
discount = 0.99
exponent_sharpness_level = 4.0
std_floor = 0.1
norm_epsilon = 1e-05

G = 64
W = 256
ONE = 56
REWARD = 57
VALUE = 58
COEF = 59
LENGTH = 60
START = 61
CHUNKS = 8
ROW_BLOCK = 416
SHORT = ROW_BLOCK
GATHERED = 512
HEAD_LIMIT = 36
BACK_LIMIT = 20

bf = functools.partial(jax.ShapeDtypeStruct, dtype=BF16)
f32 = functools.partial(jax.ShapeDtypeStruct, dtype=F32)


def dot(a, b):
    return jnp.dot(a, b, preferred_element_type=F32)


def dot_rows(a, b):
    return lax.dot_general(a, b, (((0,), (0,)), ((), ())), preferred_element_type=F32)


def split(v):
    high = v.astype(BF16)
    return high, (v - high.astype(F32)).astype(BF16)


def dot_split(high, low, w_high, w_low):
    n = high.shape[0]
    both = dot(jnp.concatenate([high, low], axis=0), w_high)
    return both[:n] + (both[n:] + dot(high, w_low))


def elu(v):
    return jnp.where(v > 0, v, jnp.exp(jnp.minimum(v, 0.0)) - 1.0)


def elu_slope(out):
    return jnp.where(out > 0, 1.0, out + 1.0)


def lanes(shape):
    return lax.broadcasted_iota(jnp.int32, shape, len(shape) - 1)


def sublanes(shape):
    return lax.broadcasted_iota(jnp.int32, shape, len(shape) - 2)


def pack_input(x):
    high = x.astype(BF16).astype(F32)
    lane = lanes(x.shape)
    low_group = (lane >= G) & (lane < 2 * G)
    return jnp.where(low_group, x - high, high).astype(BF16)


def three_groups(v):
    v = jnp.where(lanes(v.shape) < G, v, 0.0)
    return jnp.concatenate([v + pltpu.roll(v, G, 1), v], axis=1)


def padded_first(weight, bias):
    shape = (8, weight.shape[1])
    extra = jnp.where(sublanes(shape) == 0, jnp.broadcast_to(bias, shape), 0.0)
    return jnp.concatenate([weight, extra], axis=0)


def store_packed(ref, layer, full):
    high, low = split(full)
    ref[layer, 0:G, :] = high
    ref[layer, G : 2 * G, :] = high
    ref[layer, 2 * G : 3 * G, :] = low
    ref[layer, 3 * G : W, :] = jnp.zeros_like(high)


def position():
    b = lax.axis_index("batch")
    return b & 1, (b >> 1) & 1, lax.axis_index("rep")


def noise_place(n):
    return slice(n // 4 * 8, n // 4 * 8 + 8), slice(n % 4 * 128, n % 4 * 128 + 128)


def forward_kernel(
    next_ref, act_ref, obs_ref, rew_ref, val_ref, len_ref, gain_ref, noise_ref, elite_ref,
    w1_ref, b1_ref, wm_ref, bm_ref, wo_ref, bo_ref,
    xs, xc_ref, cc_ref, pt_ref, count_ref, misc_ref, noise_out, hhs, hls, mhs, mls, pulls, *refs
):
    outs, (feat, wide, line, parts), splits, sems = refs[:5], refs[5:9], refs[9:14], refs[14]
    w1p, wmh, wml, woh, wol = splits
    copies = [pltpu.make_async_copy(a, b, sems.at[n]) for n, (a, b) in enumerate(zip(splits, outs))]
    horizon, latent, slots = next_ref.shape
    width = act_ref.shape[1]
    layers = w1_ref.shape[0]

    iterations, steps, samples, _ = noise_ref.shape
    elites = elite_ref.shape[2]
    base = lax.axis_index("batch") * samples
    line[...] = jnp.zeros_like(line)
    noise_out[...] = jnp.zeros_like(noise_out)
    square = (elites, elites)
    for i in range(iterations):
        chosen = jnp.broadcast_to(elite_ref[i], square)
        mine = jnp.max(jnp.where(lanes(square) == sublanes(square), chosen, -1), axis=1, keepdims=True)
        total = jnp.zeros((elites, 128), F32)
        for t in range(steps):
            line[0:samples, 0:width] = noise_ref[i, t]
            part = jnp.zeros((elites, 128), F32)
            for j in range(samples):
                row = jnp.broadcast_to(line[j : j + 1, :], (elites, 128))
                part = part + jnp.where(mine == base + j, row, 0.0)
            total = total + (pltpu.roll(part, t * width, 1) if t else part)
        for e in range(elites // 8):
            noise_out[noise_place(i * (elites // 8) + e)] = total[e * 8 : e * 8 + 8]

    wide[...] = jnp.zeros_like(wide)
    line[...] = jnp.zeros_like(line)
    for l in range(layers):
        store_packed(w1p, l, padded_first(w1_ref[l], b1_ref[l : l + 1, :]))
        wmh[l], wml[l] = split(wm_ref[l, 0])
        for g in range(3):
            wide[g * G : g * G + latent, :] = wo_ref[:, l, :]
        woh[l], wol[l] = split(wide[...].T)
    for copy in copies:
        copy.start()
    line[...] = jnp.zeros_like(line)
    line[0:1, 0:latent] = gain_ref[...]
    line[1 : 1 + layers, 0:latent] = bo_ref[...]
    small = three_groups(line[0:8, :])
    misc_ref[slots : slots + 8, :] = small

    def turned():
        v = feat[...].T
        return jnp.concatenate([v, jnp.where(lanes(v.shape) < G, v, 0.0)], axis=1)

    feat[...] = jnp.zeros_like(feat)
    for g in range(2):
        feat[g * G : g * G + latent, :] = obs_ref[...]
    obs = turned()
    misc_ref[0:slots, :] = obs
    for g in range(2):
        feat[g * G + ONE : g * G + ONE + 1, :] = jnp.ones((1, slots), F32)

    lengths = len_ref[...].astype(F32)
    before = jnp.where(sublanes((slots, slots)) < lanes((slots, slots)), 1.0, 0.0).astype(BF16)
    starts = dot(jnp.broadcast_to(lengths, (16, slots)).astype(BF16), before)[0:1]
    count = jnp.sum(lengths, axis=1, keepdims=True)
    count_ref[...] = jnp.broadcast_to(count, count_ref.shape)
    for g in range(2):
        feat[g * G + LENGTH : g * G + LENGTH + 1, :] = lengths
        feat[g * G + START : g * G + START + 1, :] = starts
    place = lanes((slots, pt_ref.shape[1]))

    lane = lanes((slots, W))
    part = lane % G
    is_latent = (part < latent) & (lane < 3 * G)
    is_target = (lane[:, 0:128] >= REWARD) & (lane[:, 0:128] <= COEF)
    is_input = (part >= latent) & (part <= ONE) & (lane < 3 * G)

    def step(t, carry):
        z, factor = carry
        coef = jnp.where(t < len_ref[...], factor, 0.0)
        for g in range(2):
            at = g * G
            feat[at : at + latent, :] = next_ref[t]
            feat[at + latent : at + latent + width, :] = act_ref[t]
            feat[at + REWARD : at + REWARD + 1, :] = rew_ref[pl.ds(t, 1), :]
            feat[at + VALUE : at + VALUE + 1, :] = val_ref[pl.ds(t, 1), :]
            feat[at + COEF : at + COEF + 1, :] = coef
        cond = turned()
        rows = pl.ds(pl.multiple_of(t * slots, slots), slots)
        live = t.astype(F32) < cond[:, LENGTH : LENGTH + 1]
        at = jnp.where(live, cond[:, START : START + 1] + t.astype(F32), -1.0).astype(jnp.int32)
        pt_ref[rows, :] = jnp.where(place == at, 1.0, 0.0).astype(BF16)
        rest = jnp.where(is_target, cond[:, 0:128], 0.0)
        packed = 0.0
        for n in range(3):
            high = rest.astype(BF16).astype(F32)
            rest = rest - high
            packed = packed + (pltpu.roll(high, 8 * n, 1) if n else high)
        parts[rows, :] = packed.astype(BF16)
        u = jnp.where(is_input, cond, 0.0)
        for l in range(layers):
            xp = pack_input(z + u)
            xs[l, rows, :] = xp
            high, low = split(elu(dot(xp, w1p[l])))
            hhs[l, rows, :] = high
            hls[l, rows, :] = low
            high, low = split(elu(dot_split(high, low, wmh[l], wml[l]) + bm_ref[l, 0:1, :]))
            mhs[l, rows, :] = high
            mls[l, rows, :] = low
            z = z + dot_split(high, low, woh[l], wol[l]) + small[1 + l : 2 + l, :]
        scale = (2.0 * consistency_coef / latent) * cond[:, COEF : COEF + 1]
        pulls[rows, :] = jnp.where(is_latent, scale * (z - cond), 0.0)
        return z, factor * rho_decay

    lax.fori_loop(0, horizon, step, (obs * small[0:1, :], jnp.float32(1.0 / (slots * horizon))))


    def gather(top, size):
        at = slice(top, top + size)
        found = dot_rows(pt_ref[:, at], jnp.concatenate([xs[l] for l in range(layers)] + [parts[...]], axis=1))
        for l in range(layers):
            xc_ref[l, at, :] = found[:, l * W : (l + 1) * W].astype(BF16)
        values = found[:, layers * W :]
        cc_ref[at, :] = values + (pltpu.roll(values, 120, 1) + pltpu.roll(values, 112, 1))

    gather(0, GATHERED)

    @pl.when(jnp.max(count) > SHORT)
    def _():
        gather(GATHERED, pt_ref.shape[1] - GATHERED)

    for copy in copies:
        copy.wait()


def send_halves(g, keep_ref, send_ref):
    core = lax.axis_index("rep")
    half = CHUNKS // 2
    keep_ref[...] = g[:, pl.ds(core * half, half)]
    send_ref[...] = g[:, pl.ds((1 - core) * half, half)]


def weight_grads(g, layer, xp, hh, hl, dph, dpl, doh, dol, extra):
    hidden = hh.shape[1]
    grad = dot_rows(hh, dph) + (dot_rows(hl, dph) + dot_rows(hh, dpl))
    rows = hidden // CHUNKS
    for c in range(CHUNKS):
        g[layer, c, 0:rows, :] = grad[c * rows : (c + 1) * rows]
    x = xp[:, 0 : 2 * G]
    both = dot_rows(x, doh) + dot_rows(x, dol)
    first = both[0:G] + both[G : 2 * G]
    for c in range(CHUNKS):
        part = first[c * 8 : c * 8 + 8]
        g[layer, c, rows : rows + 8, :] = part if c < CHUNKS - 1 else part + extra


def turn_weights(w1_ref, b1_ref, wm_ref, wo_ref, w1th, w1tl, wmth, wmtl, wotp, wide):
    latent = wo_ref.shape[0]
    wide[...] = jnp.zeros_like(wide)
    for l in range(w1_ref.shape[0]):
        full = padded_first(w1_ref[l], b1_ref[l : l + 1, :])
        turned = jnp.concatenate([full, full, full, jnp.zeros_like(full)], axis=0).T
        w1th[l], w1tl[l] = split(turned)
        wmth[l], wmtl[l] = split(wm_ref[l, 0].T)
        wide[0:latent, :] = wo_ref[:, l, :]
        store_packed(wotp, l, wide[...])


def heads_kernel(head, has_dx, turns, *refs):
    if turns:
        *refs, wide = refs
        dynamics = refs[11 + has_dx : 15 + has_dx]
        out = len(refs) - 16 - 5
        turn_weights(*dynamics, *refs[out : out + 5], wide)
        refs = refs[:out] + refs[out + 5 :]

    (xp_ref, cond_ref, count_ref, w1_ref, b1_ref, wm_ref, bm_ref, ng_ref, nb_ref, p_ref, sb_ref) = refs[:11]
    refs = refs[11:]
    dx_in = refs[0] if has_dx else None
    refs = refs[1:] if has_dx else refs
    (
        keep_ref, send_ref, dx_ref, w1_out, wmh_out, wml_out,
        w1p, wmh, wml, w1th, w1tl, wmth, wmtl, hh, hl, dph, dpl, doh, dol, sums, g, sems,
    ) = refs[len(refs) - 22 :]
    layers = xp_ref.shape[0]
    capacity = hh.shape[1]
    short = jnp.max(count_ref[...]) <= SHORT
    blocks = jnp.where(short, SHORT // ROW_BLOCK, capacity // ROW_BLOCK)
    for l in range(layers):
        dx_ref[l, SHORT:, :] = jnp.zeros((dx_ref.shape[1] - SHORT, W), F32)
    is_reward = head == 1
    target_lane = REWARD if is_reward else VALUE
    scale = 2.0 * (reward_coef if is_reward else value_coef)
    for l in range(layers):
        full = padded_first(w1_ref[l], b1_ref[l : l + 1, :])
        store_packed(w1p, l, full)
        turned = jnp.concatenate([full, full, full, jnp.zeros_like(full)], axis=0).T
        w1th[l], w1tl[l] = split(turned)
        wm = wm_ref[l, 0]
        wmh[l], wml[l] = split(wm)
        wmth[l], wmtl[l] = split(wm.T)
    weights = [
        pltpu.make_async_copy(src, dst, sems.at[n])
        for n, (src, dst) in enumerate(((w1p, w1_out), (wmh, wmh_out), (wml, wml_out)))
    ]
    for copy in weights:
        copy.start()
    sums[...] = jnp.zeros_like(sums)

    def block(i, carry):
        rows = pl.ds(pl.multiple_of(i * ROW_BLOCK, ROW_BLOCK), ROW_BLOCK)
        kept = []
        score = 0.0
        for l in range(layers):
            o = dot(xp_ref[l, rows, :], w1p[l])
            if is_reward:
                h = elu(o)
                norm = None
            else:
                centered = o - jnp.mean(o, axis=-1, keepdims=True)
                variance = jnp.mean(centered * centered, axis=-1, keepdims=True)
                scale_rows = lax.rsqrt(variance + norm_epsilon)
                unit = centered * scale_rows
                gain = ng_ref[l, head - 2 : head - 1, :]
                h = jnp.tanh(unit * gain + nb_ref[l, head - 2 : head - 1, :])
                norm = (unit, scale_rows, gain)
            high, low = split(h)
            hh[l, rows, :] = high
            hl[l, rows, :] = low
            m = elu(dot_split(high, low, wmh[l], wml[l]) + bm_ref[l, head : head + 1, :])
            p = p_ref[head - 1, l : l + 1, :]
            score = score + jnp.sum(m * p, axis=-1, keepdims=True) + sb_ref[l, head - 1]
            kept.append((h, norm, m, p))
        cond = cond_ref[rows, :]
        miss = score - cond[:, target_lane : target_lane + 1]
        dscore = (scale * cond[:, COEF : COEF + 1]) * miss
        dscore_sum = jnp.sum(dscore, axis=0, keepdims=True)
        for l in range(layers):
            h, norm, m, p = kept[l]
            dp = jnp.sum(dscore * m, axis=0, keepdims=True)
            dpre = (dscore * p) * elu_slope(m)
            dbm = jnp.sum(dpre, axis=0, keepdims=True)
            high, low = split(dpre)
            dph[l, rows, :] = high
            dpl[l, rows, :] = low
            dh = dot_split(high, low, wmth[l], wmtl[l])
            if is_reward:
                do = dh * elu_slope(h)
            else:
                unit, scale_rows, gain = norm
                dn = dh * (1.0 - h * h)
                sums[l, 2:3, :] += jnp.sum(dn * unit, axis=0, keepdims=True)
                sums[l, 3:4, :] += jnp.sum(dn, axis=0, keepdims=True)
                dunit = dn * gain
                do = scale_rows * (
                    dunit
                    - jnp.mean(dunit, axis=-1, keepdims=True)
                    - unit * jnp.mean(dunit * unit, axis=-1, keepdims=True)
                )
            sums[l, 1:2, :] += dbm
            sums[l, 4:5, :] += dp
            sums[l, 5:6, :] += jnp.broadcast_to(dscore_sum, (1, sums.shape[2]))
            high, low = split(do)
            doh[l, rows, :] = high
            dol[l, rows, :] = low
            dx = dot_split(high, low, w1th[l], w1tl[l])
            dx_ref[l, rows, :] = dx_in[l, rows, :] + dx if has_dx else dx
        return carry

    lax.fori_loop(0, blocks, block, 0)

    def finish(n):
        for l in range(layers):
            rows = [ref[l, 0:n, :] for ref in (hh, hl, dph, dpl, doh, dol)]
            weight_grads(g, l, xp_ref[l, 0:n, :], *rows, sums[l])

    pl.when(short)(functools.partial(finish, SHORT))
    pl.when(jnp.logical_not(short))(functools.partial(finish, capacity))
    send_halves(g, keep_ref, send_ref)
    for copy in weights:
        copy.wait()


def backward_kernel(
    xp_ref, hh_ref, hl_ref, mh_ref, ml_ref, pull_ref, dx_ref, misc_ref,
    w1th, w1tl, wmth, wmtl, wotp, pt_ref, count_ref, *rest
):
    keep_ref, send_ref, dobs_ref, dxs, dph, dpl, doh, dol, dzs, sums, g = rest[len(rest) - 11 :]
    layers, rows_all = xp_ref.shape[0], xp_ref.shape[1]
    latent, slots = dobs_ref.shape
    horizon = rows_all // slots
    hidden = wmth.shape[-1]
    sums[...] = jnp.zeros_like(sums)

    def scatter(n):
        parts = [split(dx_ref[l, 0:n, :]) for l in range(layers)]
        found = dot(pt_ref[:, 0:n], jnp.concatenate([v for pair in parts for v in pair], axis=1))
        for l in range(layers):
            at = 2 * l * W
            dxs[l] = found[:, at : at + W] + found[:, at + W : at + 2 * W]

    short = jnp.max(count_ref[...]) <= SHORT
    pl.when(short)(functools.partial(scatter, GATHERED))
    pl.when(jnp.logical_not(short))(functools.partial(scatter, pt_ref.shape[1]))
    lane = lanes((slots, W))
    is_latent = ((lane % G) < latent) & (lane < 3 * G)

    def step(i, dz):
        t = horizon - 1 - i
        rows = pl.ds(pl.multiple_of(t * slots, slots), slots)
        dz = dz + pull_ref[rows, :]
        for l in reversed(range(layers)):
            dzp = pack_input(dz)
            dzs[l, rows, :] = dzp[:, 0 : 2 * G]
            sums[l, 2:3, 0:W] += jnp.sum(dz, axis=0, keepdims=True)
            m = mh_ref[l, rows, :].astype(F32) + ml_ref[l, rows, :].astype(F32)
            dpre = dot(dzp, wotp[l]) * elu_slope(m)
            sums[l, 1:2, :] += jnp.sum(dpre, axis=0, keepdims=True)
            high, low = split(dpre)
            dph[l, rows, :] = high
            dpl[l, rows, :] = low
            h = hh_ref[l, rows, :].astype(F32) + hl_ref[l, rows, :].astype(F32)
            do = dot_split(high, low, wmth[l], wmtl[l]) * elu_slope(h)
            high, low = split(do)
            doh[l, rows, :] = high
            dol[l, rows, :] = low
            dx = dot_split(high, low, w1th[l], w1tl[l]) + dxs[l, rows, :]
            dz = dz + jnp.where(is_latent, dx, 0.0)
        return dz

    dz = lax.fori_loop(0, horizon, step, jnp.zeros((slots, W), F32))
    dobs_ref[...] = (dz * misc_ref[slots : slots + 1, :])[:, 0:128].T[0:latent]
    sums[0, 3:4, 0:W] = jnp.sum(dz * misc_ref[0:slots, :], axis=0, keepdims=True)
    rows = hidden // CHUNKS
    for l in range(layers):
        weight_grads(g, l, xp_ref.at[l], hh_ref[l], hl_ref[l], dph[l], dpl[l], doh[l], dol[l], sums[l])
        both = dot_rows(dzs[l], mh_ref[l]) + dot_rows(dzs[l], ml_ref[l])
        out = both[0:G] + both[G : 2 * G]
        for c in range(CHUNKS):
            g[l, c, rows + 8 : rows + 16, :] = out[c * 8 : c * 8 + 8]
    send_halves(g, keep_ref, send_ref)


def planner_kernel(iterations, first, *refs):
    weights = refs[:14]
    state_in = refs[14:17] if first else refs[14:15]
    refs = refs[17:] if first else refs[15:]
    (noise_ref, misc_ref, bm_ref, ng_ref, nb_ref, p_ref, sb_ref) = refs[:7]
    out_ref, xs, acts, line = refs[len(refs) - 4 :]
    w1p, wmh, wml = weights[0:4], weights[4:8], weights[8:12]
    woh, wol = weights[12:14]
    horizon, elites = acts.shape[0], acts.shape[1]
    layers = w1p[0].shape[0]
    slots = misc_ref.shape[0] - 8
    latent = 50

    lane = lanes((1, W))
    is_action = ((lane % G) >= latent) & ((lane % G) < ONE) & (lane < 3 * G)
    is_one = ((lane % G) == ONE) & (lane < 3 * G)
    group = lane // G

    def placed(v, at):
        return jnp.where(is_action, three_groups(pltpu.roll(v, (latent - at) % 128, 1)), 0.0)

    def three(v):
        high = v.astype(BF16)
        rest = v - high.astype(F32)
        mid = rest.astype(BF16)
        return high, mid, (rest - mid.astype(F32)).astype(BF16)

    def dot_fine(v, w_high, w_low):
        n = v.shape[0]
        high, mid, low = three(v)
        a = dot(jnp.concatenate([high, mid, low], axis=0), w_high)
        b = dot(jnp.concatenate([high, mid], axis=0), w_low)
        return a[0:n] + (a[n : 2 * n] + b[0:n] + (a[2 * n : 3 * n] + b[n : 2 * n]))

    def dot_first(x, w):
        n = x.shape[0]
        high, mid, low = three(x)
        keep = (group == 0) | (group == 2)
        zero = jnp.zeros_like(high)
        high = jnp.where(keep, high, zero)
        mid = jnp.where(keep, mid, zero)
        low = jnp.where(group == 0, low, zero)
        a = dot(jnp.concatenate([high, mid, low], axis=0), w)
        return a[0:n] + (a[n : 2 * n] + a[2 * n : 3 * n])

    def middle(h, l, k):
        return elu(dot_fine(h, wmh[k][l], wml[k][l]) + bm_ref[l, k : k + 1, :])

    def head(m, l, k):
        return jnp.sum(m * p_ref[k - 1, l : l + 1, :], axis=-1, keepdims=True) + sb_ref[l, k - 1]

    def value(x, l, k):
        o = dot_first(x, w1p[k][l])
        centered = o - jnp.mean(o, axis=-1, keepdims=True)
        variance = jnp.mean(centered * centered, axis=-1, keepdims=True)
        unit = centered * lax.rsqrt(variance + norm_epsilon)
        h = jnp.tanh(unit * ng_ref[l, k - 2 : k - 1, :] + nb_ref[l, k - 2 : k - 1, :])
        return head(middle(h, l, k), l, k)

    if first:
        mean_ref, std_ref, start_ref = state_in
        line[...] = jnp.zeros_like(line)
        line[0:horizon, 0:6] = mean_ref[...]
        line[8 : 8 + horizon, 0:6] = std_ref[...]
        line[16:17, 0:latent] = start_ref[...]
        for t in range(horizon):
            out_ref[0, t : t + 1, :] = placed(line[t : t + 1, :], 0)
            out_ref[1, t : t + 1, :] = placed(line[8 + t : 9 + t, :], 0)
        out_ref[2, 0:1, :] = three_groups(line[16:17, :])
        state_ref = out_ref
    else:
        (state_ref,) = state_in
        out_ref[2] = state_ref[2]

    start = state_ref[2, 0:1, :]
    for iteration in iterations:
        tiles = elites // 8
        noise = [noise_ref[noise_place(iteration * tiles + e)] for e in range(tiles)]
        noise = jnp.concatenate(noise, axis=0) if tiles > 1 else noise[0]
        for t in range(horizon):
            acts[t] = jnp.where(
                is_action,
                jnp.tanh(state_ref[0, t : t + 1, :] + state_ref[1, t : t + 1, :] * placed(noise, 6 * t)),
                0.0,
            )
        z = jnp.broadcast_to(start, (elites, W))
        for t in range(horizon):
            u = jnp.where(is_one, 1.0, acts[t])
            for l in range(layers):
                x = z + u
                xs[l, t] = x
                if t < horizon - 1 or l < layers - 1:
                    m = middle(elu(dot_first(x, w1p[0][l])), l, 0)
                    z = z + dot_fine(m, woh[l], wol[l]) + misc_ref[slots + 1 + l : slots + 2 + l, :]
        reward = 0.0
        one = 0.0
        two = 0.0
        for l in range(layers):
            x = xs[l].reshape(horizon * elites, W)
            reward = reward + head(middle(elu(dot_first(x, w1p[1][l])), l, 1), l, 1)
            x = xs[l, horizon - 1]
            one = one + value(x, l, 2)
            two = two + value(x, l, 3)
        returns = discount ** (horizon - 1) * jnp.minimum(one, two)
        for t in range(horizon):
            returns = returns + discount**t * reward[t * elites : (t + 1) * elites]
        top = jnp.max(returns, axis=0, keepdims=True)
        weight = jnp.exp(exponent_sharpness_level * (returns - top))
        total = jnp.sum(weight, axis=0, keepdims=True)
        for t in range(horizon):
            sampled = acts[t]
            mean = jnp.sum(weight * sampled, axis=0, keepdims=True) / total
            centered = sampled - mean
            variance = jnp.sum(weight * (centered * centered), axis=0, keepdims=True) / total
            out_ref[0, t : t + 1, :] = mean
            out_ref[1, t : t + 1, :] = jnp.sqrt(variance + std_floor * std_floor)
        state_ref = out_ref


CORE = 0


def bits():
    x, y, _ = position()
    return ((x, y, lambda f, s: f + 2 * s), (y, x, lambda f, s: 2 * f + s))


def first_partner(l):
    return (1, 2)[l]


def second_partner(l):
    return (2, 1)[l]


def blocks(ref, rows):
    def at(n):
        return ref.at[pl.ds(n * rows, rows)]

    return at


def add_first(rows, ins, keeps, sends):
    keep, recv = (blocks(r, rows) for r in ins)
    kept = blocks(keeps[0], rows)
    for l, (f, _, chunk) in enumerate(bits()):
        sent = blocks(sends[l], rows)
        for m in range(2):
            mine, other = 4 * l + chunk(f, m), 4 * l + chunk(1 - f, m)
            kept(2 * l + m)[...] = keep(mine)[...] + recv(mine)[...]
            sent(m)[...] = keep(other)[...] + recv(other)[...]


def add_second(rows, ins, keeps, sends):
    keep, kept = blocks(ins[0], rows), blocks(keeps[0], rows)
    for l, (_, s, _) in enumerate(bits()):
        recv = blocks(ins[1 + l], rows)
        kept(l)[...] = keep(2 * l + s)[...] + recv(s)[...]
        sends[l][...] = keep(2 * l + 1 - s)[...] + recv(1 - s)[...]


def add_third(rows, ins, keeps, sends):
    for l in range(2):
        at = slice(l * rows, l * rows + rows)
        total = ins[0][at] + ins[1 + l][...]
        for ref in (*keeps, *sends):
            ref[at] = total


def add_whole(rows, ins, keeps, sends):
    total = ins[0][...]
    for ref in ins[1:]:
        total = total + ref[...]
    for ref in (*keeps, *sends):
        ref[...] = total


def add_last(rows, ins, keeps, sends):
    total = ins[0][...] + ins[1][...]
    keeps[0][...] = total
    for l in range(2):
        sends[l][...] = total[l * rows : l * rows + rows]


def join_two(rows, ins, keeps, sends):
    kept = blocks(keeps[0], rows)
    for l, (_, s, _) in enumerate(bits()):
        own, sent = ins[0][l * rows : l * rows + rows], blocks(sends[l], rows)
        recv = ins[1 + l][...]
        for at, value in ((s, own), (1 - s, recv)):
            kept(2 * l + at)[...] = value
            sent(at)[...] = value


def join_four(rows, ins, keeps, sends):
    own = blocks(ins[0], rows)
    for l, (f, _, chunk) in enumerate(bits()):
        recv = blocks(ins[1 + l], rows)
        for m in range(2):
            for at, value in ((chunk(f, m), own(2 * l + m)[...]), (chunk(1 - f, m), recv(m)[...])):
                for ref in (*keeps, *sends):
                    blocks(ref, rows)(4 * l + at)[...] = value


class Received:
    def __init__(self, buffer, start, rows):
        self.buffer, self.start, self.rows = buffer, start, rows


class Sums:
    def __init__(self, batch):
        self.batch = batch
        self.pending = []
        self.after = []
        self.late = []

    def swap(self, a, partner):
        if partner == CORE:
            return lax.ppermute(a, "rep", [(0, 1), (1, 0)])
        return lax.ppermute(a, "batch", [(i, i ^ partner) for i in range(self.batch)])

    def start(self, steps, done):
        self.pending.append([steps, done, next(steps)])

    def advance(self):
        if not self.pending:
            return
        jobs = [entry[2] for entry in self.pending]
        arrays, buffers = [], {}
        for _, _, ins, _, sends in jobs:
            for a in ins:
                a = a.buffer if isinstance(a, Received) else a
                if not any(a is b for b in arrays):
                    arrays.append(a)
            for partner, rows in sends:
                buffers[partner] = buffers.get(partner, 0) + rows
        partners = list(buffers)
        width = jobs[0][2][0].shape[-1]
        out_shape = [f32((n, width)) for _, _, _, keeps, _ in jobs for n in keeps]
        out_shape += [f32((buffers[p], width)) for p in partners] + [f32((8, 128))]
        after = self.after + self.late

        def kernel(*refs):
            ins_all, outs = refs[: len(arrays)], list(refs[len(arrays) + len(after) :])
            outs.pop()[...] = jnp.zeros((8, 128), F32)
            sent_refs = dict(zip(partners, outs[len(outs) - len(partners) :]))
            used = dict.fromkeys(partners, 0)
            for fn, rows, ins, keeps, sends in jobs:
                in_refs = []
                for a in ins:
                    whole = a.buffer if isinstance(a, Received) else a
                    ref = ins_all[[whole is b for b in arrays].index(True)]
                    in_refs.append(ref.at[pl.ds(a.start, a.rows)] if isinstance(a, Received) else ref)
                sent = []
                for partner, n in sends:
                    sent.append(sent_refs[partner].at[pl.ds(used[partner], n)])
                    used[partner] += n
                fn(rows, in_refs, outs[: len(keeps)], sent)
                outs = outs[len(keeps) :]

        outs = pl.pallas_call(
            kernel,
            in_specs=[vmem()] * len(arrays) + [hbm()] * len(after),
            out_specs=[vmem()] * len(out_shape),
            out_shape=out_shape,
            compiler_params=params(20),
            cost_estimate=cost(6),
            name="add_up",
        )(*arrays, *after)
        token = outs[-1]
        received = {p: self.swap(a, p) for p, a in zip(partners, outs[len(outs) - 1 - len(partners) :])}
        used = dict.fromkeys(partners, 0)
        self.late = []
        for entry, (_, _, _, keeps, sends) in zip(list(self.pending), jobs):
            result = list(outs[: len(keeps)])
            outs = outs[len(keeps) :]
            for partner, n in sends:
                result.append(Received(received[partner], used[partner], n))
                used[partner] += n
            try:
                entry[2] = entry[0].send(result)
            except StopIteration as stop:
                self.pending.remove(entry)
                entry[1].append(stop.value)
                if isinstance(stop.value[-1], Received):
                    self.late.append(stop.value[-1].buffer)
        self.after = [token]

    def sum_small(self, a):
        rows, bit, steps = a.shape[0], 8, []
        while bit < self.batch:
            steps.append(bit)
            bit *= 2
        steps += [1, 2, 4][: 3 if self.batch > 4 else 2]
        recv = self.swap(a, steps[0])
        for partner in steps[1:]:
            a, recv = yield (add_whole, rows, (a, recv), (rows,), ((partner, rows),))
        (a,) = yield (add_whole, rows, (a, recv), (rows,), ())
        return (a,)

    def sum_batch(self, keep, send):
        _, _, rows, hidden = keep.shape
        keep, send = keep.reshape(-1, hidden), send.reshape(-1, hidden)
        to_first = tuple((first_partner(l), 2 * rows) for l in range(2))
        to_second = tuple((second_partner(l), rows) for l in range(2))
        keep, ra, rb = yield (add_first, rows, (keep, self.swap(send, CORE)), (4 * rows,), to_first)
        keep, ra, rb = yield (add_second, rows, (keep, ra, rb), (2 * rows,), to_second)
        keep, recv = yield (add_third, rows, (keep, ra, rb), (2 * rows,), ((4, 2 * rows),))
        bit = 8
        while bit < self.batch:
            keep, recv = yield (add_whole, rows, (keep, recv), (2 * rows,), ((bit, 2 * rows),))
            bit *= 2
        keep, ra, rb = yield (add_last, rows, (keep, recv), (2 * rows,), to_second)
        keep, ra, rb = yield (join_two, rows, (keep, ra, rb), (4 * rows,), to_first)
        keep, recv = yield (join_four, rows, (keep, ra, rb), (8 * rows,), ((CORE, 8 * rows),))
        return rows, keep, recv


def vmem():
    return pl.BlockSpec(memory_space=pltpu.VMEM)


def smem():
    return pl.BlockSpec(memory_space=pltpu.SMEM)


def hbm():
    return pl.BlockSpec(memory_space=pl.ANY)


def params(mebibytes):
    return pltpu.CompilerParams(vmem_limit_bytes=mebibytes * 1024 * 1024)


def in_hbm(a):
    return pltpu.with_memory_space_constraint(a, pltpu.HBM)


def cost(us):
    return pl.CostEstimate(flops=int(us * 1e9), bytes_accessed=0, transcendentals=0)


def shape_of(a):
    return jax.ShapeDtypeStruct(a.shape, a.dtype)


def assemble_kernel(hidden, latent, batches, *refs):
    half = CHUNKS // 2
    parts, heights = {}, {}
    for n, (k, height, start) in enumerate(batches):
        parts[k] = [refs[2 * n], refs[2 * n + 1].at[pl.ds(start, height * CHUNKS)]]
        heights[k] = height
    last = 0 in parts
    core = lax.axis_index("rep")
    rows = hidden // CHUNKS
    copies = []
    if last:
        small_in, dobs_in = refs[2 * len(batches) + 2 : 2 * len(batches) + 4]
        (
            mid_ref, first_ref, bias_ref, mid_bias_ref, ng_ref, nb_ref, wo_ref, bo_ref, p_ref, sb_ref, gain_ref,
            dobs_ref, sems,
        ) = refs[len(refs) - 13 :]
        dobs_ref[...] = dobs_in[...]
    else:
        mid_ref, first_ref, small_ref, sems = refs[len(refs) - 4 :]

    def copy(src, dst, sem, when=None):
        made = pltpu.make_async_copy(src, dst, sem)
        if when is None:
            made.start()
        else:
            pl.when(when)(made.start)
        return made

    for k in parts:
        at = pl.ds(k * hidden, hidden)
        for l in range(2):
            for m, owner in ((0, core), (1, 1 - core)):
                for j in range(half):
                    top = (l * half + j) * heights[k]
                    src = parts[k][m].at[pl.ds(top, rows)]
                    copies.append(copy(src, mid_ref.at[l, k, owner * half + j], sems.at[0, k, l, m, j]))
                    rest = parts[k][m].at[pl.ds(top + rows, 8)]
                    lower = copy(rest, first_ref.at[l, j, :, at], sems.at[1, k, l, 0, j], owner == 0)
                    if m == 0:
                        copies.append(lower)
                    if j < half - 1:
                        upper = copy(rest, first_ref.at[l, half + j, :, at], sems.at[1, k, l, 1, j], owner == 1)
                        if m == 0:
                            copies.append(upper)

    def chunk(k, l, c, lo, hi):
        top = (l * half + c % half) * heights[k] + rows
        own, other = (parts[k][m][top + lo : top + hi, :] for m in range(2))
        return jnp.where(core == c // half, own, other)

    if last:
        for l in range(2):
            for k in range(4):
                small = chunk(k, l, CHUNKS - 1, 0, 8) if k in parts else small_in[k, l]
                bias_ref[l : l + 1, k * hidden : (k + 1) * hidden] = small[0:1]
                mid_bias_ref[l, k : k + 1, :] = small[1:2]
                if k >= 1:
                    p_ref[k - 1, l : l + 1, :] = small[4:5]
                    sb_ref[l : l + 1, k - 1 : k] = small[5:6, 0:1]
                if k >= 2:
                    ng_ref[l, k - 2 : k - 1, :] = small[2:3]
                    nb_ref[l, k - 2 : k - 1, :] = small[3:4]
                if k == 0:
                    bo_ref[l : l + 1, :] = small[2:3, 0:latent]
                    if l == 0:
                        gain_ref[...] = small[3:4, 0:latent]
            for c in range(CHUNKS - 1):
                n = min(8, latent - 8 * c)
                wo_ref[8 * c : 8 * c + n, l, :] = chunk(0, l, c, 8, 8 + n)
    else:
        small_ref[...] = jnp.zeros_like(small_ref)
        for k in parts:
            for l in range(2):
                small_ref[k, l] = chunk(k, l, CHUNKS - 1, 0, 8)
    for made in copies:
        made.wait()


def shards(
    obs_latent, actions, next_latent, reward_target, value_target, lengths,
    first_weight, opening_layer_offset, mid_weight, mid_bias, norm_gain, norm_bias,
    latent_out, latent_bias, payoff_critic_projection, scalar_bias, obs_gain,
    plan_start, action_guess_average, plan_init_std, action_noise, elite_index,
    *, batch,
):
    slots, latent = obs_latent.shape
    horizon, width = actions.shape[1], actions.shape[2]
    layers, hidden = first_weight.shape[0], mid_weight.shape[-1]
    rows_all = slots * horizon
    joint = latent + width
    iterations, samples_local, plan_horizon = action_noise.shape[1:4]
    elites = elite_index.shape[-1]
    heads = 3
    sums = Sums(batch)

    projection = jnp.transpose(payoff_critic_projection, (1, 0, 2))
    wout = jnp.transpose(latent_out, (2, 0, 1))

    def column(k):
        return [
            pl.BlockSpec((layers, joint, hidden), lambda i: (0, 0, k)),
            pl.BlockSpec((layers, hidden), lambda i: (0, k)),
            pl.BlockSpec((layers, 1, hidden, hidden), lambda i: (0, k, 0, 0)),
        ]

    def scratch(*shape, dtype=BF16):
        return pltpu.VMEM(shape, dtype)

    def copies(*shapes):
        return [scratch(*v.shape, dtype=v.dtype) for v in shapes]

    def to_hbm(*shapes):
        return [pltpu.HBM(v.shape, v.dtype) for v in shapes]

    def weights_of(*arrays):
        return [in_hbm(a) for a in arrays]

    square = bf((layers, hidden, hidden))
    narrow = bf((layers, hidden, W))
    packed = bf((layers, W, hidden))
    wide_rows = bf((layers, rows_all, hidden))
    noise_shape = f32((8 * -(-iterations * (elites // 8) // 4), hidden))
    kept = [packed, square, square, narrow, narrow]
    capacity = -(-rows_all // ROW_BLOCK) * ROW_BLOCK
    gathered = -(-capacity // 128) * 128
    (xp, xc, cc, pt, live_count, misc, noise, hh, hl, mh, ml, pull, w1p, wmh, wml, woh, wol) = pl.pallas_call(
        forward_kernel,
        grid=(1,),
        in_specs=[vmem()] * 9 + column(0) + [vmem()] * 3,
        out_specs=[vmem()] * 12 + [hbm()] * 5,
        out_shape=[
            bf((layers, rows_all, W)), bf((layers, gathered, W)), f32((gathered, 128)), bf((rows_all, gathered)),
            f32((8, 128)), f32((slots + 8, W)), noise_shape,
            *[wide_rows] * 4, f32((rows_all, W)), *to_hbm(*kept),
        ],
        scratch_shapes=[
            scratch(2 * G, slots, dtype=F32),
            scratch(W, hidden, dtype=F32),
            scratch(max(8, samples_local), 128, dtype=F32),
            scratch(rows_all, 128),
            *copies(*kept),
            pltpu.SemaphoreType.DMA((5,)),
        ],
        compiler_params=params(26),
        cost_estimate=cost(20),
        name="forward_chain",
    )(
        *weights_of(
            jnp.transpose(next_latent, (1, 2, 0)), jnp.transpose(actions, (1, 2, 0)), obs_latent.T,
            reward_target.T, value_target.T, lengths[None], obs_gain[None],
            jnp.transpose(action_noise[0], (0, 2, 1, 3)), jnp.transpose(elite_index, (1, 0, 2)),
            first_weight, opening_layer_offset, mid_weight, mid_bias, wout, latent_bias,
        )
    )
    noise_done = []
    split_weights = [(w1p, wmh, wml)]

    summed = [[] for _ in range(4)]
    dx = None
    rows = hidden // CHUNKS + 8
    half = f32((layers, CHUNKS // 2, rows, hidden))
    for head in range(1, 1 + heads):
        has_dx = dx is not None
        turns = head == heads
        keep, send, dx, *weights = pl.pallas_call(
            functools.partial(heads_kernel, head, has_dx, turns),
            grid=(1,),
            in_specs=[vmem()] * 3 + column(head) + [vmem()] * 4 + [smem()] + [vmem()] * has_dx
            + (column(0) + [vmem()] if turns else []) + [hbm()] * len(sums.after),
            out_specs=[vmem()] * 3 + [hbm()] * 3 + [vmem()] * (5 * turns),
            out_shape=[half, half, f32((layers, gathered, W)), *to_hbm(packed, square, square)]
            + [narrow, narrow, square, square, packed] * turns,
            scratch_shapes=[
                *copies(packed, square, square, narrow, narrow, square, square),
                *[scratch(layers, capacity, hidden)] * 6,
                scratch(layers, 8, hidden, dtype=F32),
                scratch(layers, CHUNKS, rows, hidden, dtype=F32),
                pltpu.SemaphoreType.DMA((3,)),
                *[scratch(G, hidden, dtype=F32)] * turns,
            ],
            compiler_params=params(HEAD_LIMIT),
            cost_estimate=cost(15),
            name=f"head_{head}",
        )(
            xc, cc, live_count,
            *weights_of(
                first_weight, opening_layer_offset, mid_weight, mid_bias,
                norm_gain, norm_bias, projection, scalar_bias,
            ),
            *([dx] if has_dx else []),
            *(weights_of(first_weight, opening_layer_offset, mid_weight, wout) if turns else []), *sums.after,
        )
        split_weights.append(tuple(weights[:3]))
        turned = weights[3:]
        sums.after = [dx]
        sums.advance()
        sums.start(sums.sum_batch(keep, send), summed[head])
        if head == 1:
            sums.start(sums.sum_small(noise), noise_done)

    rows = hidden // CHUNKS + 16
    half = f32((layers, CHUNKS // 2, rows, hidden))
    keep, send, dobs = pl.pallas_call(
        backward_kernel,
        grid=(1,),
        in_specs=[vmem()] * 15 + [hbm()] * len(sums.after),
        out_specs=[vmem()] * 3,
        out_shape=[half, half, f32((latent, slots))],
        scratch_shapes=[
            scratch(layers, rows_all, W, dtype=F32),
            *[scratch(layers, rows_all, hidden)] * 4,
            scratch(layers, rows_all, 2 * G),
            scratch(layers, 8, hidden, dtype=F32),
            scratch(layers, CHUNKS, rows, hidden, dtype=F32),
        ],
        compiler_params=params(BACK_LIMIT),
        cost_estimate=cost(25),
        name="backward_chain",
    )(xp, hh, hl, mh, ml, pull, dx, misc, *turned, pt, live_count, *sums.after)
    sums.after = [dobs]
    sums.advance()
    sums.start(sums.sum_batch(keep, send), summed[0])

    while not noise_done:
        sums.advance()
    ((noise,),) = noise_done
    flat_weights = [w[n] for n in range(3) for w in split_weights] + [woh, wol]
    state = [action_guess_average[0], plan_init_std[0], plan_start]
    groups = [[i] for i in range(iterations)]
    if iterations > 5:
        groups[3:5] = [groups[3] + groups[4]]
    for group in groups:
        i = group[0]
        state = [
            pl.pallas_call(
                functools.partial(planner_kernel, group, i == 0),
                in_specs=[vmem()] * (14 + len(state)) + [vmem()] * 6 + [smem()]
                + [hbm()] * len(sums.after),
                out_specs=vmem(),
                out_shape=f32((3, plan_horizon, W)),
                scratch_shapes=[
                    scratch(layers, plan_horizon, elites, W, dtype=F32),
                    scratch(plan_horizon, elites, W, dtype=F32),
                    scratch(24, 128, dtype=F32),
                ],
                compiler_params=params(20),
                cost_estimate=cost(9 * len(group)),
                name=f"planner_{i}",
            )(
                *flat_weights, *state, noise, misc, mid_bias, norm_gain, norm_bias, projection,
                scalar_bias, *sums.after,
            )
        ]
        sums.after = [state[0]]
        sums.advance()
    plan = state[0][:2, None, :, latent:joint]
    big = [
        f32((layers, 4, CHUNKS, hidden // CHUNKS, hidden)), f32((layers, CHUNKS - 1, 8, 4 * hidden)),
    ]

    def assemble(heads_done, more, out_shape, aliases, name, after):
        done = [(k, *summed[k][0]) for k in heads_done]
        pieces = [p for _, _, own, other in done for p in (own, other.buffer)]
        spec = tuple((k, rows, other.start) for k, rows, _, other in done)
        return pl.pallas_call(
            functools.partial(assemble_kernel, hidden, latent, spec),
            in_specs=[vmem()] * len(pieces) + [hbm(), hbm(), vmem(), vmem()][: len(more)] + [hbm()] * len(after),
            out_specs=[hbm(), hbm()] + [vmem()] * (len(out_shape) - 2),
            out_shape=out_shape,
            scratch_shapes=[pltpu.SemaphoreType.DMA((2, 4, 2, 2, CHUNKS // 2))],
            input_output_aliases={len(pieces) + n: n for n in range(2)} if aliases else {},
            compiler_params=params(24),
            cost_estimate=cost(3),
            name=name,
        )(*pieces, *more, *after)

    early = [k for k in range(4) if summed[k]]
    held = assemble(early, [], big + [f32((4, layers, 8, hidden))], False, "assemble_early", sums.after)
    sums.after = [held[2]]
    while sums.pending:
        sums.advance()
    late = [k for k in range(4) if k not in early]
    mids, firsts, *outs = assemble(
        late,
        [*held, dobs],
        big
        + [
            f32(opening_layer_offset.shape), f32(mid_bias.shape), f32(norm_gain.shape), f32(norm_bias.shape),
            f32(wout.shape), f32(latent_bias.shape), f32(projection.shape), f32(scalar_bias.shape), f32((1, latent)),
            f32(dobs.shape),
        ],
        True,
        "assemble",
        sums.after,
    )
    return (
        firsts.reshape(first_weight.shape),
        outs[0],
        mids.reshape(mid_weight.shape),
        *outs[1:4],
        jnp.transpose(outs[4], (1, 2, 0)),
        outs[5],
        jnp.transpose(outs[6], (1, 0, 2)),
        outs[7],
        outs[8][0],
        outs[9].T,
        plan[0],
        plan[1],
    )


def solution(mesh):
    rows = ("batch", "rep")
    return jax.shard_map(
        functools.partial(shards, batch=mesh.shape["batch"]),
        mesh=mesh,
        in_specs=(
            P(rows, None), P(rows, None, None), P(rows, None, None), P(rows, None), P(rows, None), P(rows),
            P(), P(), P(), P(), P(), P(), P(), P(), P(), P(), P(),
            P("rep", None), P("rep", None, None), P("rep", None, None),
            P("rep", None, "batch", None, None), P("rep", None, None),
        ),
        out_specs=(P(),) * 11 + (P(rows, None), P("rep", None, None), P("rep", None, None)),
        check_vma=False,
    )
```
